128 devices in a mesh: nodes: 128 (over x, y, z, core).
Axes of the slice: x: 4, y: 4, z: 4, core: 2. Of those that a mesh axis runs over, the one named last changes fastest.
Arguments:
- features: bfloat16 [262144, 128], P('nodes'), may hold values from -6 to 6
- weight: bfloat16 [128, 256], replicated, may hold values from -0.5 to 0.5
- cotangent: bfloat16 [262144, 256], P('nodes'), may hold values from -6 to 6
- block_pairs: int32 [12288, 2], P('nodes'), may hold values from 0 to 1023, as said below
- tile_counts: int32 [128], P('nodes'), may hold values from 48 to 96, as said below
- tile_values: bfloat16 [12288, 256, 256], P('nodes'), may hold values from -0.125 to 0.125
Outputs:
- hidden: bfloat16 [262144, 256], P('nodes')
- weight_grad: float32 [128, 256], replicated
- feature_grad: bfloat16 [262144, 128], P('nodes')
The draws below stay inside these ranges and needn't reach their ends.
Inputs may be any that keep to these rules, and one draw needn't show every extreme that they name: `block_pairs`: every live slot of device d has its row block homed on d. Live slots of one device name at most one column block homed on any other device, and some device names blocks of min(72, 128 - 1) other devices. Slots after the live ones hold the pair (d * 8, d * 8). `tile_counts`: some device in every draw has all 96 slots live.
All inputs are finite; a program needn't handle non-finite values.
Results may differ from the reference program's by a relative error of at most 0.0075.
Values may be sent and summed in bfloat16 or wider, within the bound.
No kernel may reach another device: no remote copies, remote signals or barrier semaphores. Data moves between devices by JAX's collectives and lax.ppermute only.
A program may use at most 192 MiB of HBM per device.

```python
import jax
import jax.numpy as jnp
from jax import lax

B = 256
F = 128
HID = 256
NB = 8
MAXP = 96
BLOCKS = 1024
NODES = 262144
SLOTS = 12288
N_NODES = 128


def pair_layout(key):
    peers_total = N_NODES
    keys = jax.random.split(key, 6)
    lowest = MAXP // 2
    level = jax.random.randint(keys[0], (peers_total,), 0, 64)
    counts_drawn = lowest + (MAXP - lowest) * level * level // (63 * 63)
    busiest = jax.random.randint(keys[1], (), 0, peers_total)
    device_ids = jnp.arange(peers_total, dtype=jnp.int32)
    counts_drawn = jnp.where(device_ids == busiest, MAXP, counts_drawn).astype(jnp.int32)
    remote_total = jnp.minimum(counts_drawn - counts_drawn // 4, peers_total - 1)
    orders = jax.vmap(lambda sub_key: jax.random.permutation(sub_key, peers_total - 1))(jax.random.split(keys[2], peers_total))
    slot_ids = jnp.arange(MAXP, dtype=jnp.int32)
    offsets = orders[:, slot_ids % (peers_total - 1)] + 1
    peer_ids = (device_ids[:, None] + offsets) % peers_total
    is_remote = slot_ids[None, :] < remote_total[:, None]
    live = slot_ids[None, :] < counts_drawn[:, None]
    row_blocks = device_ids[:, None] * NB + jax.random.randint(keys[3], (peers_total, MAXP), 0, NB)
    far_blocks = peer_ids * NB + jax.random.randint(keys[4], (peers_total, MAXP), 0, NB)
    near_blocks = device_ids[:, None] * NB + jax.random.randint(keys[5], (peers_total, MAXP), 0, NB)
    col_blocks = jnp.where(is_remote, far_blocks, near_blocks)
    own_first = jnp.broadcast_to(device_ids[:, None] * NB, (peers_total, MAXP))
    row_blocks = jnp.where(live, row_blocks, own_first)
    col_blocks = jnp.where(live, col_blocks, own_first)
    pair_table = jnp.stack([row_blocks, col_blocks], -1).reshape(peers_total * MAXP, 2).astype(jnp.int32)
    return (counts_drawn, pair_table)


def draw_block_pairs(key, part):
    counts_drawn, pair_table = pair_layout(key)
    return pair_table


def draw_tile_counts(key, part):
    counts_drawn, pair_table = pair_layout(key)
    return counts_drawn


def block_levels(key, dims, cuts, least, largest):
    def one(axis_at, shards_of):
        draws = jax.random.uniform(jax.random.fold_in(jax.random.fold_in(key, 6), axis_at), (shards_of,), jnp.float32, least / len(cuts), largest / len(cuts))
        return jnp.repeat(jnp.exp(draws), dims[axis_at] // shards_of).reshape((-1,) + (1,) * (len(dims) - axis_at - 1))

    level = one(*cuts[0])
    for cut in cuts[1:]:
        level = level * one(*cut)
    return level


def noise(own_key, extent, scale, limit, pieces=(), kind=jnp.bfloat16):
    entries = scale * jax.random.normal(own_key, extent, jnp.float32)
    if pieces:
        entries = entries * block_levels(own_key, extent, pieces, -0.22, 0.18)
    return jnp.clip(entries, -limit, limit).astype(kind)


def setup_inputs(seed: int = 0) -> dict:
    key_of = jax.random.split(jax.random.key(seed), 7)
    features = noise(key_of[0], (NODES, F), 1.0, 6.0, ((0, 128),))
    weight = noise(key_of[1], (F, HID), F ** -0.5, 0.5)
    cotangent = noise(key_of[2], (NODES, HID), 1.0, 6.0, ((0, 128),))
    block_pairs = draw_block_pairs(jax.random.fold_in(key_of[6], 71), 0)
    tile_counts = draw_tile_counts(jax.random.fold_in(key_of[6], 71), 0)
    tile_values = noise(key_of[5], (SLOTS, B, B), (8 * B) ** -0.5, 0.125, ((0, 128),))
    return {"features": features, "weight": weight, "cotangent": cotangent, "block_pairs": block_pairs, "tile_counts": tile_counts, "tile_values": tile_values}


def aggregate(values, tile_values, block_pairs, tile_counts):
    blocks = values.reshape(BLOCKS, B, F)
    tile_sets = tile_values.reshape(N_NODES, MAXP, B, B)
    pair_sets = block_pairs.reshape(N_NODES, MAXP, 2).astype(jnp.int32)

    def visit(totals, element):
        tile_set, pair_set, count_now = element
        row_blocks = pair_set[:, 0]
        col_blocks = pair_set[:, 1]
        tiles_wide = tile_set.astype(jnp.float32)
        direct = jnp.einsum('jab,jbf->jaf', tiles_wide, blocks[col_blocks].astype(jnp.float32), precision=lax.Precision.HIGHEST)
        transposed = jnp.einsum('jab,jaf->jbf', tiles_wide, blocks[row_blocks].astype(jnp.float32), precision=lax.Precision.HIGHEST)
        rounded = lax.optimization_barrier(transposed.astype(jnp.bfloat16)).astype(jnp.float32)
        remote = col_blocks // NB != row_blocks // NB
        transposed = jnp.where(remote[:, None, None], rounded, transposed)
        live = (jnp.arange(MAXP, dtype=jnp.int32) < count_now)[:, None, None]
        totals = totals.at[row_blocks].add(jnp.where(live, direct, jnp.float32(0)))
        totals = totals.at[col_blocks].add(jnp.where(live, transposed, jnp.float32(0)))
        return (totals, None)
    start = jnp.zeros((BLOCKS, B, F), jnp.float32)
    totals, unused = lax.scan(visit, start, (tile_sets, pair_sets, tile_counts.astype(jnp.int32)))
    return totals.reshape(NODES, F)

def reference(features, weight, cotangent, block_pairs, tile_counts, tile_values):
    aggregated = aggregate(features, tile_values, block_pairs, tile_counts).astype(jnp.bfloat16)
    preact = jnp.dot(aggregated, weight, preferred_element_type=jnp.float32)
    hidden = jax.nn.silu(preact).astype(jnp.bfloat16)
    sigma = jax.nn.sigmoid(preact)
    delta = (cotangent.astype(jnp.float32) * sigma * (1.0 + preact * (1.0 - sigma))).astype(jnp.bfloat16)
    weight_grad = jnp.dot(aggregated.T, delta, preferred_element_type=jnp.float32) / jnp.sqrt(jnp.float32(NODES))
    upstream = jnp.dot(delta, weight.T, preferred_element_type=jnp.float32).astype(jnp.bfloat16)
    feature_grad = aggregate(upstream, tile_values, block_pairs, tile_counts).astype(jnp.bfloat16)
    return (hidden, weight_grad, feature_grad)
```

```python
import functools
import math

import jax
import jax.numpy as jnp
from jax import lax
from jax.experimental import pallas as pl
from jax.experimental.pallas import tpu as pltpu
from jax.sharding import PartitionSpec as P

VMEM_LIMIT = 60 * 1024 * 1024
GROUP = 16
PARTS = 4
EXTRA = 16
TWICE = 64


def whole(*shape):
    return pl.BlockSpec(shape, lambda *_: (0,) * len(shape), pipeline_mode=pl.Buffered(1))


def params(limit=VMEM_LIMIT):
    return pltpu.CompilerParams(vmem_limit_bytes=limit)


def send_blocks(asked_ref, blocks_ref, out_ref, sems):
    def copy(q):
        block = jnp.maximum(asked_ref[q], 0)
        return pltpu.make_async_copy(blocks_ref.at[block], out_ref.at[q], sems.at[q])

    def start(q, carry):
        @pl.when(asked_ref[q] >= 0)
        def _():
            copy(q).start()

        return carry

    def wait(q, carry):
        @pl.when(asked_ref[q] >= 0)
        def _():
            copy(q).wait()

        return carry

    peers = asked_ref.shape[0]
    lax.fori_loop(0, peers, start, 0)
    lax.fori_loop(0, peers, wait, 0)


def pick(asked, blocks):
    peers = asked.shape[0]
    locals_, rows, width = blocks.shape
    return pl.pallas_call(
        send_blocks,
        grid_spec=pltpu.PrefetchScalarGridSpec(
            num_scalar_prefetch=1,
            grid=(1,),
            in_specs=[whole(locals_, rows, width)],
            out_specs=pl.BlockSpec(memory_space=pl.ANY),
            scratch_shapes=[pltpu.SemaphoreType.DMA((peers,))],
        ),
        out_shape=jax.ShapeDtypeStruct((peers, rows, width), blocks.dtype),
        compiler_params=params(),
    )(asked, blocks)


def transposed_kernel(
    peers, row_ref, dest_ref, again_ref, blocks_ref, tiles_ref, out_ref, total_ref
):
    step = pl.program_id(0)

    @pl.when(step == 0)
    def _():
        total_ref[...] = jnp.zeros_like(total_ref)

    def visit(at, carry):
        slot = step * GROUP + at
        dest = dest_ref[slot]

        @pl.when(dest >= 0)
        def _():
            row = row_ref[slot]
            product = lax.dot_general(
                tiles_ref[at],
                blocks_ref[row],
                (((0,), (0,)), ((), ())),
                preferred_element_type=jnp.float32,
            )
            remote = dest < peers

            @pl.when(remote & (again_ref[slot] == 0))
            def _():
                out_ref[dest] = product.astype(out_ref.dtype)

            @pl.when(remote & (again_ref[slot] == 1))
            def _():
                out_ref[dest] = (out_ref[dest].astype(jnp.float32) + product).astype(out_ref.dtype)

            @pl.when(jnp.logical_not(remote))
            def _():
                column = dest - peers
                total_ref[column] += product
                total_ref[row] += jnp.dot(
                    tiles_ref[at], blocks_ref[column], preferred_element_type=jnp.float32
                )

        return carry

    lax.fori_loop(0, GROUP, visit, 0)


def transposed_products(row_local, dest, again, blocks, tile_values, peers):
    slots, rows, _ = tile_values.shape
    locals_, _, width = blocks.shape
    return pl.pallas_call(
        functools.partial(transposed_kernel, peers),
        grid_spec=pltpu.PrefetchScalarGridSpec(
            num_scalar_prefetch=3,
            grid=(slots // GROUP,),
            in_specs=[
                whole(locals_, rows, width),
                pl.BlockSpec((GROUP, rows, rows), lambda i, *_: (i, 0, 0)),
            ],
            out_specs=[whole(peers, rows, width), whole(locals_, rows, width)],
        ),
        out_shape=[
            jax.ShapeDtypeStruct((peers, rows, width), blocks.dtype),
            jax.ShapeDtypeStruct((locals_, rows, width), jnp.float32),
        ],
        compiler_params=params(),
        cost_estimate=pl.CostEstimate(
            flops=3 * slots * rows * rows * width, bytes_accessed=24 << 20, transcendentals=0
        ),
    )(row_local, dest, again, blocks, tile_values)


def direct_kernel(peers, row_ref, dest_ref, arrived_ref, tiles_ref, start_ref, total_ref):
    step = pl.program_id(0)

    @pl.when(step == 0)
    def _():
        total_ref[...] = start_ref[...]

    def visit(at, carry):
        slot = step * GROUP + at
        source = dest_ref[slot]

        @pl.when((source >= 0) & (source < peers))
        def _():
            total_ref[row_ref[slot]] += jnp.dot(
                tiles_ref[at], arrived_ref[source], preferred_element_type=jnp.float32
            )

        return carry

    lax.fori_loop(0, GROUP, visit, 0)


def direct_products(row_local, dest, arrived, tile_values, start):
    slots, rows, _ = tile_values.shape
    peers, _, width = arrived.shape
    locals_ = start.shape[0]
    return pl.pallas_call(
        functools.partial(direct_kernel, peers),
        grid_spec=pltpu.PrefetchScalarGridSpec(
            num_scalar_prefetch=2,
            grid=(slots // GROUP,),
            in_specs=[
                whole(peers, rows, width),
                pl.BlockSpec((GROUP, rows, rows), lambda i, *_: (i, 0, 0)),
                whole(locals_, rows, width),
            ],
            out_specs=whole(locals_, rows, width),
        ),
        out_shape=jax.ShapeDtypeStruct((locals_, rows, width), jnp.float32),
        compiler_params=params(),
        cost_estimate=pl.CostEstimate(
            flops=2 * slots * rows * rows * width, bytes_accessed=24 << 20, transcendentals=0
        ),
    )(row_local, dest, arrived, tile_values, start)


def add_returned(asked_ref, returned_ref, start_ref, total_ref, landed_ref, sems):
    def copy(q):
        return pltpu.make_async_copy(returned_ref.at[q], landed_ref.at[q], sems.at[q])

    def start(q, carry):
        @pl.when(asked_ref[q] >= 0)
        def _():
            copy(q).start()

        return carry

    def add(q, carry):
        block = asked_ref[q]

        @pl.when(block >= 0)
        def _():
            copy(q).wait()
            total_ref[block] += landed_ref[q].astype(jnp.float32)

        return carry

    peers = asked_ref.shape[0]
    lax.fori_loop(0, peers, start, 0)
    total_ref[...] = start_ref[...]
    lax.fori_loop(0, peers, add, 0)


def dense_kernel(
    asked_ref,
    returned_ref,
    start_ref,
    weight_ref,
    cotangent_ref,
    hidden_ref,
    grad_ref,
    upstream_ref,
    out_ref,
    total_ref,
    landed_ref,
    sems,
):
    add_returned(asked_ref, returned_ref, start_ref, total_ref, landed_ref, sems)
    grad_ref[...] = jnp.zeros_like(grad_ref)
    weight = weight_ref[...]

    def block_step(k, carry):
        aggregated = total_ref[k].astype(jnp.bfloat16)
        preact = jnp.dot(aggregated, weight, preferred_element_type=jnp.float32)
        sigma = 1.0 / (1.0 + jnp.exp(-preact))
        hidden_ref[k] = (preact * sigma).astype(jnp.bfloat16)
        delta = (
            cotangent_ref[k].astype(jnp.float32) * sigma * (1.0 + preact * (1.0 - sigma))
        ).astype(jnp.bfloat16)
        grad_ref[...] += lax.dot_general(
            aggregated, delta, (((0,), (0,)), ((), ())), preferred_element_type=jnp.float32
        )
        upstream_ref[k] = lax.dot_general(
            delta, weight, (((1,), (1,)), ((), ())), preferred_element_type=jnp.float32
        ).astype(jnp.bfloat16)
        return carry

    lax.fori_loop(0, total_ref.shape[0], block_step, 0)
    send_blocks(asked_ref, upstream_ref, out_ref, sems)


def dense(asked, returned, start, weight, cotangent):
    peers, rows, width = returned.shape
    locals_ = start.shape[0]
    hid = weight.shape[1]
    return pl.pallas_call(
        dense_kernel,
        grid_spec=pltpu.PrefetchScalarGridSpec(
            num_scalar_prefetch=1,
            grid=(1,),
            in_specs=[
                pl.BlockSpec(memory_space=pl.ANY),
                whole(locals_, rows, width),
                whole(width, hid),
                whole(locals_, rows, hid),
            ],
            out_specs=[
                whole(locals_, rows, hid),
                whole(width, hid),
                whole(locals_, rows, width),
                pl.BlockSpec(memory_space=pl.ANY),
            ],
            scratch_shapes=[
                pltpu.VMEM((locals_, rows, width), jnp.float32),
                pltpu.VMEM((peers, rows, width), returned.dtype),
                pltpu.SemaphoreType.DMA((peers,)),
            ],
        ),
        out_shape=[
            jax.ShapeDtypeStruct((locals_, rows, hid), jnp.bfloat16),
            jax.ShapeDtypeStruct((width, hid), jnp.float32),
            jax.ShapeDtypeStruct((locals_, rows, width), jnp.bfloat16),
            jax.ShapeDtypeStruct((peers, rows, width), jnp.bfloat16),
        ],
        compiler_params=params(),
    )(asked, returned, start, weight, cotangent)


def finish_kernel(asked_ref, returned_ref, start_ref, out_ref, total_ref, landed_ref, sems):
    add_returned(asked_ref, returned_ref, start_ref, total_ref, landed_ref, sems)
    out_ref[...] = total_ref[...].astype(out_ref.dtype)


def finish(asked, returned, start):
    peers, rows, width = returned.shape
    locals_ = start.shape[0]
    return pl.pallas_call(
        finish_kernel,
        grid_spec=pltpu.PrefetchScalarGridSpec(
            num_scalar_prefetch=1,
            grid=(1,),
            in_specs=[pl.BlockSpec(memory_space=pl.ANY), whole(locals_, rows, width)],
            out_specs=whole(locals_, rows, width),
            scratch_shapes=[
                pltpu.VMEM((locals_, rows, width), jnp.float32),
                pltpu.VMEM((peers, rows, width), returned.dtype),
                pltpu.SemaphoreType.DMA((peers,)),
            ],
        ),
        out_shape=jax.ShapeDtypeStruct((locals_, rows, width), jnp.bfloat16),
        compiler_params=params(),
    )(asked, returned, start)


def exchange(values):
    return lax.all_to_all(values, "nodes", split_axis=0, concat_axis=0, tiled=True)


ASKED, VIA, RELAYED, CAME_VIA, WANTED, FITS = range(6)
OPEN = -2


def plan_kernel(me_ref, wanted_ref, plan_ref, free_ref, rows_ref, columns_ref):
    peers = wanted_ref.shape[0]
    me = me_ref[0]
    raw = wanted_ref[...]
    u_ids = lax.broadcasted_iota(jnp.int32, raw.shape, 0)
    v_ids = lax.broadcasted_iota(jnp.int32, raw.shape, 1)
    named = (raw >= 0).astype(jnp.float32)
    flipped = named.T
    skewed = flipped
    for bit in range(peers.bit_length() - 1):
        turned = pltpu.roll(skewed, peers - (1 << bit), 1)
        skewed = jnp.where(((u_ids >> bit) & 1) == 1, turned, skewed)
    free_ref[...] = (1.0 - skewed.T).astype(jnp.int32)
    route = jnp.where((named > 0) & (flipped > 0), OPEN, -1)
    spare = 1 - flipped.astype(jnp.int32)

    def left_open(route):
        return jnp.sum((route == OPEN).astype(jnp.float32)).astype(jnp.int32)

    def one(turn, carry):
        route, spare = carry
        fits = (route == OPEN) & ((spare & free_ref[pl.ds(turn, 1), :]) > 0)
        first = jnp.min(jnp.where(fits, u_ids, peers), axis=0, keepdims=True)
        chosen = fits & (u_ids == first)
        route = jnp.where(chosen, (v_ids + turn) & (peers - 1), route)
        spare = jnp.where(chosen, 0, spare)
        return route, pltpu.roll(spare, peers - 1, 1)

    def some(carry):
        turn, _, route, spare = carry
        route, spare = lax.fori_loop(0, 8, lambda i, c: one(turn + i, c), (route, spare))
        return turn + 8, left_open(route), route, spare

    _, left, route, _ = lax.while_loop(
        lambda carry: (carry[0] < peers) & (carry[1] > 0),
        some,
        (jnp.int32(0), left_open(route), route, spare),
    )
    rows_ref[...] = route
    columns_ref[...] = route.astype(jnp.float32).T.astype(jnp.int32)
    plan_ref[VIA : VIA + 1, :] = rows_ref[pl.ds(me, 1), :]
    plan_ref[CAME_VIA : CAME_VIA + 1, :] = columns_ref[pl.ds(me, 1), :]
    plan_ref[RELAYED : RELAYED + 1, :] = jnp.max(
        jnp.where(route == me, u_ids, -1), axis=0, keepdims=True
    )
    columns_ref[...] = raw.astype(jnp.float32).T.astype(jnp.int32)
    plan_ref[ASKED : ASKED + 1, :] = columns_ref[pl.ds(me, 1), :]
    plan_ref[WANTED : WANTED + 1, :] = wanted_ref[pl.ds(me, 1), :]
    twice = jnp.sum((raw >= TWICE).astype(jnp.float32)).astype(jnp.int32)
    fits = jnp.where((left == 0) & (twice == 0), 1, 0)
    plan_ref[FITS:, :] = jnp.full((plan_ref.shape[0] - FITS, peers), fits, jnp.int32)


def make_plan(myself, wanted):
    peers = wanted.shape[0]
    square = pltpu.VMEM((peers, peers), jnp.int32)
    return pl.pallas_call(
        plan_kernel,
        grid_spec=pltpu.PrefetchScalarGridSpec(
            num_scalar_prefetch=1,
            grid=(1,),
            in_specs=[whole(peers, peers)],
            out_specs=whole(8, peers),
            scratch_shapes=[square, square, square],
        ),
        out_shape=jax.ShapeDtypeStruct((8, peers), jnp.int32),
        compiler_params=params(),
    )(jnp.full((1,), myself, jnp.int32), wanted)


def each_peer(peers, act):
    def step(q, carry):
        act(q)
        return carry

    lax.fori_loop(0, peers, step, 0, unroll=8)


def send_first(plan_ref, blocks_ref, out_ref, sems):
    peers = plan_ref.shape[1]
    half = blocks_ref.shape[1] // 2

    def direct(q):
        block = jnp.maximum(plan_ref[ASKED, q], 0)
        return pltpu.make_async_copy(
            blocks_ref.at[block, pl.ds(0, half)], out_ref.at[q, pl.ds(0, half)], sems.at[q]
        )

    def relayed(q):
        block = jnp.maximum(plan_ref[ASKED, q], 0)
        via = jnp.maximum(plan_ref[VIA, q], 0)
        return pltpu.make_async_copy(
            blocks_ref.at[block, pl.ds(half, half)],
            out_ref.at[via, pl.ds(0, half)],
            sems.at[peers + q],
        )

    def start(q):
        @pl.when(plan_ref[ASKED, q] >= 0)
        def _():
            direct(q).start()

        @pl.when(plan_ref[VIA, q] >= 0)
        def _():
            relayed(q).start()

    def wait(q):
        @pl.when(plan_ref[ASKED, q] >= 0)
        def _():
            direct(q).wait()

        @pl.when(plan_ref[VIA, q] >= 0)
        def _():
            relayed(q).wait()

    each_peer(peers, start)
    each_peer(peers, wait)


def first_halves(plan, blocks):
    peers = plan.shape[1]
    locals_, rows, width = blocks.shape
    return pl.pallas_call(
        send_first,
        grid_spec=pltpu.PrefetchScalarGridSpec(
            num_scalar_prefetch=1,
            grid=(1,),
            in_specs=[whole(locals_, rows, width)],
            out_specs=pl.BlockSpec(memory_space=pl.ANY),
            scratch_shapes=[pltpu.SemaphoreType.DMA((2 * peers,))],
        ),
        out_shape=jax.ShapeDtypeStruct((peers, rows // 2, width), blocks.dtype),
        compiler_params=params(),
    )(plan, blocks)


def tiles_spec(rows):
    return pl.BlockSpec(
        (GROUP, rows, rows), lambda i, plan, slots: (jnp.minimum(i, slots[3, 0]), 0, 0)
    )


ROW, HOME, COLUMN, LAST = range(4)


def products_kernel(plan_ref, slots_ref, blocks_ref, tiles_ref, out_ref, total_ref):
    step = pl.program_id(0)
    peers = plan_ref.shape[1]
    rows = blocks_ref.shape[1]
    half = rows // 2
    locals_ = blocks_ref.shape[0]

    @pl.when(step == 0)
    def _():
        total_ref[...] = jnp.zeros_like(total_ref)

        def second_half(q):
            @pl.when((plan_ref[ASKED, q] >= 0) & (plan_ref[WANTED, q] < 0))
            def _():
                out_ref[q, pl.ds(0, half)] = blocks_ref[plan_ref[ASKED, q], pl.ds(half, half)]

        each_peer(peers, second_half)

    @pl.when(step <= slots_ref[LAST, 0])
    def _():
        for at in range(GROUP):
            slot = step * GROUP + at
            row, home, column = slots_ref[ROW, slot], slots_ref[HOME, slot], slots_ref[COLUMN, slot]
            tile = tiles_ref[at]
            product = lax.dot_general(
                tile, blocks_ref[row], (((0,), (0,)), ((), ())), preferred_element_type=jnp.float32
            )
            out_ref[home, pl.ds(0, rows)] = product.astype(out_ref.dtype)

            @pl.when(column < locals_)
            def _():
                total_ref[column] += product
                total_ref[row] += jnp.dot(
                    tile, blocks_ref[column], preferred_element_type=jnp.float32
                )


def own_products(plan, slots, blocks, tile_values, extra):
    peers = plan.shape[1]
    slot_total, rows, _ = tile_values.shape
    locals_, _, width = blocks.shape
    return pl.pallas_call(
        products_kernel,
        grid_spec=pltpu.PrefetchScalarGridSpec(
            num_scalar_prefetch=2,
            grid=(slot_total // GROUP,),
            in_specs=[whole(locals_, rows, width), tiles_spec(rows)],
            out_specs=[whole(peers, rows + extra, width), whole(locals_, rows, width)],
        ),
        out_shape=[
            jax.ShapeDtypeStruct((peers, rows + extra, width), blocks.dtype),
            jax.ShapeDtypeStruct((locals_, rows, width), jnp.float32),
        ],
        compiler_params=params(),
        cost_estimate=pl.CostEstimate(
            flops=3 * slot_total * rows * rows * width, bytes_accessed=24 << 20, transcendentals=0
        ),
    )(plan, slots, blocks, tile_values)


def three_parts(value):
    high = value.astype(jnp.bfloat16)
    rest = value - high.astype(jnp.float32)
    middle = rest.astype(jnp.bfloat16)
    low = (rest - middle.astype(jnp.float32)).astype(jnp.bfloat16)
    return [part.astype(jnp.float32) for part in (high, middle, low)]


def relay_kernel(plan_ref, came_ref, _, out_ref, held_ref, sems, *grad_refs):
    peers = plan_ref.shape[1]
    half = came_ref.shape[1] - (EXTRA if grad_refs else 0)

    def take(q):
        source = jnp.maximum(plan_ref[RELAYED, q], 0)
        return pltpu.make_async_copy(
            came_ref.at[source, pl.ds(0, half)], held_ref.at[q], sems.at[q]
        )

    def give(q):
        return pltpu.make_async_copy(
            held_ref.at[q], out_ref.at[q, pl.ds(half, half)], sems.at[peers + q]
        )

    def start(q):
        @pl.when(plan_ref[RELAYED, q] >= 0)
        def _():
            take(q).start()

    def turn(q):
        @pl.when(plan_ref[RELAYED, q] >= 0)
        def _():
            take(q).wait()
            give(q).start()

    def wait(q):
        @pl.when(plan_ref[RELAYED, q] >= 0)
        def _():
            give(q).wait()

    if grad_refs:
        (staged_ref,) = grad_refs
        bring = pltpu.make_async_copy(
            came_ref.at[:, pl.ds(half, EXTRA)], staged_ref, sems.at[2 * peers]
        )
        bring.start()
    each_peer(peers, start)
    if grad_refs:
        bring.wait()
        sums = jnp.sum(staged_ref[...].astype(jnp.float32), axis=0)
        own = (sums[4:6] + sums[2:4]) + sums[0:2]
        parts = three_parts(own)
        packed = jnp.concatenate(parts + [jnp.zeros((EXTRA - 6, own.shape[1]), jnp.float32)], 0)
        staged_ref[...] = jnp.broadcast_to(packed[None], staged_ref.shape).astype(jnp.bfloat16)
        put = pltpu.make_async_copy(
            staged_ref, out_ref.at[:, pl.ds(2 * half, EXTRA)], sems.at[2 * peers + 1]
        )
        put.start()
    each_peer(peers, turn)
    if grad_refs:
        put.wait()
    each_peer(peers, wait)


def relay(plan, came, outgoing, with_grad):
    peers, _, width = came.shape
    scratch = [
        pltpu.VMEM((peers, came.shape[1] - (EXTRA if with_grad else 0), width), came.dtype),
        pltpu.SemaphoreType.DMA((2 * peers + 2,)),
    ]
    if with_grad:
        scratch.append(pltpu.VMEM((peers, EXTRA, width), jnp.bfloat16))
    anywhere = pl.BlockSpec(memory_space=pl.ANY)
    return pl.pallas_call(
        relay_kernel,
        grid_spec=pltpu.PrefetchScalarGridSpec(
            num_scalar_prefetch=1,
            grid=(1,),
            in_specs=[anywhere, anywhere],
            out_specs=anywhere,
            scratch_shapes=scratch,
        ),
        out_shape=jax.ShapeDtypeStruct(outgoing.shape, outgoing.dtype),
        input_output_aliases={2: 0},
        compiler_params=params(),
    )(plan, came, outgoing)


def early_kernel(plan_ref, slots_ref, first_ref, tiles_ref, start_ref, total_ref, sums_ref):
    step = pl.program_id(0)
    half = tiles_ref.shape[2]
    locals_ = start_ref.shape[0]

    @pl.when(step == 0)
    def _():
        sums_ref[pl.ds(0, locals_)] = start_ref[...]

    @pl.when(step <= slots_ref[LAST, 0])
    def _():
        for at in range(GROUP):
            slot = step * GROUP + at
            remote = slots_ref[COLUMN, slot] == locals_
            row = jnp.where(remote, slots_ref[ROW, slot], locals_)
            sums_ref[row] += jnp.dot(
                tiles_ref[at],
                first_ref[slots_ref[HOME, slot], pl.ds(0, half)],
                preferred_element_type=jnp.float32,
            )

    @pl.when(step == pl.num_programs(0) - 1)
    def _():
        total_ref[...] = sums_ref[pl.ds(0, locals_)]


def early_products(plan, slots, first, tile_values, start):
    slot_total, rows, _ = tile_values.shape
    locals_, _, width = start.shape
    return pl.pallas_call(
        early_kernel,
        grid_spec=pltpu.PrefetchScalarGridSpec(
            num_scalar_prefetch=2,
            grid=(slot_total // GROUP,),
            in_specs=[
                whole(*first.shape),
                pl.BlockSpec(
                    (GROUP, rows, rows // 2),
                    lambda i, plan, slots: (jnp.minimum(i, slots[LAST, 0]), 0, 0),
                ),
                whole(*start.shape),
            ],
            out_specs=whole(*start.shape),
            scratch_shapes=[pltpu.VMEM((locals_ + 1, rows, width), jnp.float32)],
        ),
        out_shape=jax.ShapeDtypeStruct(start.shape, start.dtype),
        compiler_params=params(),
        cost_estimate=pl.CostEstimate(
            flops=slot_total * rows * rows * width, bytes_accessed=12 << 20, transcendentals=0
        ),
    )(plan, slots, first, tile_values, start)


def late_scratch(second, tile_values, start):
    peers, _, width = second.shape
    slot_total, rows, _ = tile_values.shape
    return [
        pltpu.VMEM((start.shape[0] + 1, rows, width), jnp.float32),
        pltpu.VMEM(second.shape, second.dtype),
        pltpu.VMEM((slot_total, rows, rows // 2), tile_values.dtype),
        pltpu.SemaphoreType.DMA((PARTS + slot_total // GROUP,)),
    ]


def late_sums(plan_ref, slots_ref, second_ref, tiles_ref, start_ref, total_ref, landed_ref, held_ref, sems):
    peers = plan_ref.shape[1]
    slot_total, rows, half = held_ref.shape
    locals_ = start_ref.shape[0]
    share = peers // PARTS

    def landing(part):
        piece = pl.ds(part * share, share)
        return pltpu.make_async_copy(second_ref.at[piece], landed_ref.at[piece], sems.at[part])

    def holding(group):
        piece = pl.ds(group * GROUP, GROUP)
        return pltpu.make_async_copy(
            tiles_ref.at[piece, :, pl.ds(half, half)], held_ref.at[piece], sems.at[PARTS + group]
        )

    for part in range(PARTS):
        landing(part).start()
    groups = slot_total // GROUP
    for group in range(groups):

        @pl.when(group <= slots_ref[LAST, 0])
        def _():
            holding(group).start()

    total_ref[pl.ds(0, locals_)] = start_ref[...]

    def add(q, carry):
        block = plan_ref[ASKED, q]

        @pl.when(block >= 0)
        def _():
            total_ref[block] += landed_ref[q, pl.ds(0, rows)].astype(jnp.float32)

        return carry

    for part in range(PARTS):
        landing(part).wait()
        lax.fori_loop(part * share, (part + 1) * share, add, 0, unroll=4)

    def multiply(group, carry):
        @pl.when(group <= slots_ref[LAST, 0])
        def _():
            holding(group).wait()
            for at in range(GROUP):
                slot = group * GROUP + at
                home = slots_ref[HOME, slot]
                remote = slots_ref[COLUMN, slot] == locals_
                row = jnp.where(remote, slots_ref[ROW, slot], locals_)
                via = plan_ref[CAME_VIA, home]
                source = jnp.where(via >= 0, via, home)
                offset = pl.multiple_of(jnp.where(via >= 0, half, 0), half)
                total_ref[row] += jnp.dot(
                    held_ref[slot],
                    landed_ref[source, pl.ds(offset, half)],
                    preferred_element_type=jnp.float32,
                )

        return carry

    lax.fori_loop(0, groups, multiply, 0)


def layer_kernel(
    plan_ref,
    slots_ref,
    second_ref,
    tiles_ref,
    start_ref,
    weight_ref,
    cotangent_ref,
    hidden_ref,
    upstream_ref,
    out_ref,
    total_ref,
    landed_ref,
    held_ref,
    late_sems,
    grad_ref,
    rows_ref,
    staged_ref,
    sems,
):
    late_sums(
        plan_ref,
        slots_ref,
        second_ref,
        tiles_ref,
        start_ref,
        total_ref,
        landed_ref,
        held_ref,
        late_sems,
    )
    peers = plan_ref.shape[1]
    half = held_ref.shape[2]
    width = upstream_ref.shape[2]
    weight = weight_ref[...]
    grad_ref[...] = jnp.zeros_like(grad_ref)

    def block_step(k, carry):
        aggregated = total_ref[k].astype(jnp.bfloat16)
        preact = jnp.dot(aggregated, weight, preferred_element_type=jnp.float32)
        sigma = 1.0 / (1.0 + jnp.exp(-preact))
        hidden_ref[k] = (preact * sigma).astype(jnp.bfloat16)
        delta = (
            cotangent_ref[k].astype(jnp.float32) * sigma * (1.0 + preact * (1.0 - sigma))
        ).astype(jnp.bfloat16)
        grad_ref[...] += lax.dot_general(
            aggregated, delta, (((0,), (0,)), ((), ())), preferred_element_type=jnp.float32
        )
        upstream_ref[k] = lax.dot_general(
            delta, weight, (((1,), (1,)), ((), ())), preferred_element_type=jnp.float32
        ).astype(jnp.bfloat16)
        return carry

    lax.fori_loop(0, cotangent_ref.shape[0], block_step, 0, unroll=2)
    for side in range(2):
        parts = three_parts(grad_ref[:, side * width : (side + 1) * width])
        for at, part in enumerate(parts):
            rows_ref[:, 2 * at + side, :] = part
    for at in range(6, EXTRA):
        rows_ref[:, at, :] = jnp.zeros((peers, width), jnp.float32)
    staged_ref[...] = rows_ref[...].astype(jnp.bfloat16)
    put = pltpu.make_async_copy(staged_ref, out_ref.at[:, pl.ds(half, EXTRA)], sems.at[2 * peers])
    put.start()
    send_first(plan_ref, upstream_ref, out_ref, sems)
    put.wait()


def layer(plan, slots, second, tile_values, start, weight, cotangent):
    peers, _, width = second.shape
    _, rows, _ = tile_values.shape
    locals_ = start.shape[0]
    hid = weight.shape[1]
    assert width == peers and hid == 2 * width
    anywhere = pl.BlockSpec(memory_space=pl.ANY)
    return pl.pallas_call(
        layer_kernel,
        grid_spec=pltpu.PrefetchScalarGridSpec(
            num_scalar_prefetch=2,
            grid=(1,),
            in_specs=[
                anywhere,
                anywhere,
                whole(*start.shape),
                whole(width, hid),
                whole(locals_, rows, hid),
            ],
            out_specs=[whole(locals_, rows, hid), whole(locals_, rows, width), anywhere],
            scratch_shapes=late_scratch(second, tile_values, start)
            + [
                pltpu.VMEM((width, hid), jnp.float32),
                pltpu.VMEM((peers, EXTRA, width), jnp.float32),
                pltpu.VMEM((peers, EXTRA, width), jnp.bfloat16),
                pltpu.SemaphoreType.DMA((2 * peers + 1,)),
            ],
        ),
        out_shape=[
            jax.ShapeDtypeStruct((locals_, rows, hid), jnp.bfloat16),
            jax.ShapeDtypeStruct((locals_, rows, width), jnp.bfloat16),
            jax.ShapeDtypeStruct((peers, rows // 2 + EXTRA, width), jnp.bfloat16),
        ],
        compiler_params=params(),
    )(plan, slots, second, tile_values, start, weight, cotangent)


def last_kernel(
    scale,
    plan_ref,
    slots_ref,
    second_ref,
    tiles_ref,
    start_ref,
    out_ref,
    weight_grad_ref,
    total_ref,
    landed_ref,
    held_ref,
    late_sems,
    rows_ref,
):
    late_sums(
        plan_ref,
        slots_ref,
        second_ref,
        tiles_ref,
        start_ref,
        total_ref,
        landed_ref,
        held_ref,
        late_sems,
    )
    rows = held_ref.shape[1]
    width = out_ref.shape[2]
    out_ref[...] = total_ref[pl.ds(0, out_ref.shape[0])].astype(out_ref.dtype)
    rows_ref[...] = landed_ref[:, pl.ds(rows, EXTRA)].astype(jnp.float32)
    for side in range(2):
        weight_grad_ref[:, side * width : (side + 1) * width] = (
            rows_ref[:, 4 + side, :] + rows_ref[:, 2 + side, :] + rows_ref[:, side, :]
        ) * scale


def last(plan, slots, second, tile_values, start, scale):
    peers, _, width = second.shape
    _, rows, _ = tile_values.shape
    locals_ = start.shape[0]
    anywhere = pl.BlockSpec(memory_space=pl.ANY)
    return pl.pallas_call(
        functools.partial(last_kernel, scale),
        grid_spec=pltpu.PrefetchScalarGridSpec(
            num_scalar_prefetch=2,
            grid=(1,),
            in_specs=[anywhere, anywhere, whole(*start.shape)],
            out_specs=[whole(locals_, rows, width), whole(peers, 2 * width)],
            scratch_shapes=late_scratch(second, tile_values, start)
            + [pltpu.VMEM((peers, EXTRA, width), jnp.float32)],
        ),
        out_shape=[
            jax.ShapeDtypeStruct((locals_, rows, width), jnp.bfloat16),
            jax.ShapeDtypeStruct((peers, 2 * width), jnp.float32),
        ],
        compiler_params=params(),
    )(plan, slots, second, tile_values, start)


def on_device(features, weight, cotangent, block_pairs, tile_counts, tile_values):
    peers = lax.axis_size("nodes")
    myself = lax.axis_index("nodes")
    rows = tile_values.shape[1]
    width = features.shape[1]
    hid = weight.shape[1]
    locals_ = features.shape[0] // rows
    count = tile_counts[0]
    slot_ids = jnp.arange(block_pairs.shape[0], dtype=jnp.int32)
    peer_ids = jnp.arange(peers, dtype=jnp.int32)
    row_local = jnp.clip(block_pairs[:, 0] - myself * locals_, 0, locals_ - 1)
    col_blocks = block_pairs[:, 1]
    home = col_blocks // locals_
    column = col_blocks % locals_
    live = slot_ids < count
    remote = live & (home != myself)
    hit = (home[None, :] == peer_ids[:, None]) & remote[None, :]
    wanted = jnp.max(jnp.where(hit, column[None, :], -1), axis=1)
    named_twice = jnp.sum(hit.astype(jnp.int32), axis=1) > 1
    wanted = wanted + jnp.where(named_twice, TWICE, 0)
    everyones = exchange(jnp.broadcast_to(wanted[None, :], (peers, peers)))
    plan = make_plan(myself, everyones)
    blocks = features.reshape(locals_, rows, width)
    cotangent_blocks = cotangent.reshape(locals_, rows, hid)
    scale = 1.0 / math.sqrt(peers * locals_ * rows)

    def sparse():
        slots = jnp.stack(
            [
                row_local,
                jnp.where(remote, home, myself),
                jnp.where(live & ~remote, column, jnp.where(remote, locals_, locals_ + 1)),
                jnp.broadcast_to((count - 1) // GROUP, row_local.shape),
            ]
        )
        first = exchange(first_halves(plan, blocks))
        outgoing, total = own_products(plan, slots, blocks, tile_values, 0)
        first, outgoing = lax.optimization_barrier((first, outgoing))
        second = exchange(relay(plan, first, outgoing, False))
        total = early_products(plan, slots, first, tile_values, total)
        hidden, upstream, sending = layer(
            plan, slots, second, tile_values, total, weight, cotangent_blocks
        )
        first = exchange(sending)
        outgoing, total = own_products(plan, slots, upstream, tile_values, EXTRA)
        first, outgoing = lax.optimization_barrier((first, outgoing))
        second = exchange(relay(plan, first, outgoing, True))
        total = early_products(plan, slots, first, tile_values, total)
        feature_grad, weight_grad = last(plan, slots, second, tile_values, total, scale)
        return hidden, weight_grad, feature_grad

    def full():
        asked = plan[ASKED]
        asked = jnp.where(asked >= 0, asked % TWICE, -1)
        dest = jnp.where(live, jnp.where(remote, home, peers + column), -1)
        earlier = (home[None, :] == home[:, None]) & (slot_ids[None, :] < slot_ids[:, None])
        again = jnp.any(earlier, axis=1).astype(jnp.int32)
        arrived = exchange(pick(asked, blocks))
        outgoing, total = transposed_products(row_local, dest, again, blocks, tile_values, peers)
        returned = exchange(outgoing)
        total = direct_products(row_local, dest, arrived, tile_values, total)
        hidden, local_grad, upstream, sending = dense(
            asked, returned, total, weight, cotangent_blocks
        )
        weight_grad = lax.psum(local_grad, "nodes") * scale
        arrived = exchange(sending)
        outgoing, total = transposed_products(row_local, dest, again, upstream, tile_values, peers)
        returned = exchange(outgoing)
        total = direct_products(row_local, dest, arrived, tile_values, total)
        return hidden, weight_grad, finish(asked, returned, total)

    hidden, weight_grad, feature_grad = lax.cond(plan[FITS, 0] > 0, sparse, full)
    return (
        hidden.reshape(locals_ * rows, hid),
        weight_grad,
        feature_grad.reshape(locals_ * rows, width),
    )


def solution(mesh):
    return jax.shard_map(
        on_device,
        mesh=mesh,
        in_specs=(
            P("nodes", None),
            P(),
            P("nodes", None),
            P("nodes", None),
            P("nodes"),
            P("nodes", None, None),
        ),
        out_specs=(P("nodes", None), P(), P("nodes", None)),
        check_vma=False,
    )
```

```python
import functools
import math

import jax
import jax.numpy as jnp
from jax import lax
from jax.experimental import pallas as pl
from jax.experimental.pallas import tpu as pltpu
from jax.sharding import PartitionSpec as P

VMEM_LIMIT = 60 * 1024 * 1024
GROUP = 16
PARTS = 4
EXTRA = 16
TWICE = 64
TURNS = 8


def whole(*shape):
    return pl.BlockSpec(shape, lambda *_: (0,) * len(shape), pipeline_mode=pl.Buffered(1))


def params(limit=VMEM_LIMIT):
    return pltpu.CompilerParams(vmem_limit_bytes=limit)


def send_blocks(asked_ref, blocks_ref, out_ref, sems):
    def copy(q):
        block = jnp.maximum(asked_ref[q], 0)
        return pltpu.make_async_copy(blocks_ref.at[block], out_ref.at[q], sems.at[q])

    def start(q, carry):
        @pl.when(asked_ref[q] >= 0)
        def _():
            copy(q).start()

        return carry

    def wait(q, carry):
        @pl.when(asked_ref[q] >= 0)
        def _():
            copy(q).wait()

        return carry

    peers = asked_ref.shape[0]
    lax.fori_loop(0, peers, start, 0)
    lax.fori_loop(0, peers, wait, 0)


def pick(asked, blocks):
    peers = asked.shape[0]
    locals_, rows, width = blocks.shape
    return pl.pallas_call(
        send_blocks,
        grid_spec=pltpu.PrefetchScalarGridSpec(
            num_scalar_prefetch=1,
            grid=(1,),
            in_specs=[whole(locals_, rows, width)],
            out_specs=pl.BlockSpec(memory_space=pl.ANY),
            scratch_shapes=[pltpu.SemaphoreType.DMA((peers,))],
        ),
        out_shape=jax.ShapeDtypeStruct((peers, rows, width), blocks.dtype),
        compiler_params=params(),
    )(asked, blocks)


def transposed_kernel(
    peers, row_ref, dest_ref, again_ref, blocks_ref, tiles_ref, out_ref, total_ref
):
    step = pl.program_id(0)

    @pl.when(step == 0)
    def _():
        total_ref[...] = jnp.zeros_like(total_ref)

    def visit(at, carry):
        slot = step * GROUP + at
        dest = dest_ref[slot]

        @pl.when(dest >= 0)
        def _():
            row = row_ref[slot]
            product = lax.dot_general(
                tiles_ref[at],
                blocks_ref[row],
                (((0,), (0,)), ((), ())),
                preferred_element_type=jnp.float32,
            )
            remote = dest < peers

            @pl.when(remote & (again_ref[slot] == 0))
            def _():
                out_ref[dest] = product.astype(out_ref.dtype)

            @pl.when(remote & (again_ref[slot] == 1))
            def _():
                out_ref[dest] = (out_ref[dest].astype(jnp.float32) + product).astype(out_ref.dtype)

            @pl.when(jnp.logical_not(remote))
            def _():
                column = dest - peers
                total_ref[column] += product
                total_ref[row] += jnp.dot(
                    tiles_ref[at], blocks_ref[column], preferred_element_type=jnp.float32
                )

        return carry

    lax.fori_loop(0, GROUP, visit, 0)


def transposed_products(row_local, dest, again, blocks, tile_values, peers):
    slots, rows, _ = tile_values.shape
    locals_, _, width = blocks.shape
    return pl.pallas_call(
        functools.partial(transposed_kernel, peers),
        grid_spec=pltpu.PrefetchScalarGridSpec(
            num_scalar_prefetch=3,
            grid=(slots // GROUP,),
            in_specs=[
                whole(locals_, rows, width),
                pl.BlockSpec((GROUP, rows, rows), lambda i, *_: (i, 0, 0)),
            ],
            out_specs=[whole(peers, rows, width), whole(locals_, rows, width)],
        ),
        out_shape=[
            jax.ShapeDtypeStruct((peers, rows, width), blocks.dtype),
            jax.ShapeDtypeStruct((locals_, rows, width), jnp.float32),
        ],
        compiler_params=params(),
        cost_estimate=pl.CostEstimate(
            flops=3 * slots * rows * rows * width, bytes_accessed=24 << 20, transcendentals=0
        ),
    )(row_local, dest, again, blocks, tile_values)


def direct_kernel(peers, row_ref, dest_ref, arrived_ref, tiles_ref, start_ref, total_ref):
    step = pl.program_id(0)

    @pl.when(step == 0)
    def _():
        total_ref[...] = start_ref[...]

    def visit(at, carry):
        slot = step * GROUP + at
        source = dest_ref[slot]

        @pl.when((source >= 0) & (source < peers))
        def _():
            total_ref[row_ref[slot]] += jnp.dot(
                tiles_ref[at], arrived_ref[source], preferred_element_type=jnp.float32
            )

        return carry

    lax.fori_loop(0, GROUP, visit, 0)


def direct_products(row_local, dest, arrived, tile_values, start):
    slots, rows, _ = tile_values.shape
    peers, _, width = arrived.shape
    locals_ = start.shape[0]
    return pl.pallas_call(
        functools.partial(direct_kernel, peers),
        grid_spec=pltpu.PrefetchScalarGridSpec(
            num_scalar_prefetch=2,
            grid=(slots // GROUP,),
            in_specs=[
                whole(peers, rows, width),
                pl.BlockSpec((GROUP, rows, rows), lambda i, *_: (i, 0, 0)),
                whole(locals_, rows, width),
            ],
            out_specs=whole(locals_, rows, width),
        ),
        out_shape=jax.ShapeDtypeStruct((locals_, rows, width), jnp.float32),
        compiler_params=params(),
        cost_estimate=pl.CostEstimate(
            flops=2 * slots * rows * rows * width, bytes_accessed=24 << 20, transcendentals=0
        ),
    )(row_local, dest, arrived, tile_values, start)


def add_returned(asked_ref, returned_ref, start_ref, total_ref, landed_ref, sems):
    def copy(q):
        return pltpu.make_async_copy(returned_ref.at[q], landed_ref.at[q], sems.at[q])

    def start(q, carry):
        @pl.when(asked_ref[q] >= 0)
        def _():
            copy(q).start()

        return carry

    def add(q, carry):
        block = asked_ref[q]

        @pl.when(block >= 0)
        def _():
            copy(q).wait()
            total_ref[block] += landed_ref[q].astype(jnp.float32)

        return carry

    peers = asked_ref.shape[0]
    lax.fori_loop(0, peers, start, 0)
    total_ref[...] = start_ref[...]
    lax.fori_loop(0, peers, add, 0)


def dense_kernel(
    asked_ref,
    returned_ref,
    start_ref,
    weight_ref,
    cotangent_ref,
    hidden_ref,
    grad_ref,
    upstream_ref,
    out_ref,
    total_ref,
    landed_ref,
    sems,
):
    add_returned(asked_ref, returned_ref, start_ref, total_ref, landed_ref, sems)
    grad_ref[...] = jnp.zeros_like(grad_ref)
    weight = weight_ref[...]

    def block_step(k, carry):
        aggregated = total_ref[k].astype(jnp.bfloat16)
        preact = jnp.dot(aggregated, weight, preferred_element_type=jnp.float32)
        sigma = 1.0 / (1.0 + jnp.exp(-preact))
        hidden_ref[k] = (preact * sigma).astype(jnp.bfloat16)
        delta = (
            cotangent_ref[k].astype(jnp.float32) * sigma * (1.0 + preact * (1.0 - sigma))
        ).astype(jnp.bfloat16)
        grad_ref[...] += lax.dot_general(
            aggregated, delta, (((0,), (0,)), ((), ())), preferred_element_type=jnp.float32
        )
        upstream_ref[k] = lax.dot_general(
            delta, weight, (((1,), (1,)), ((), ())), preferred_element_type=jnp.float32
        ).astype(jnp.bfloat16)
        return carry

    lax.fori_loop(0, total_ref.shape[0], block_step, 0)
    send_blocks(asked_ref, upstream_ref, out_ref, sems)


def dense(asked, returned, start, weight, cotangent):
    peers, rows, width = returned.shape
    locals_ = start.shape[0]
    hid = weight.shape[1]
    return pl.pallas_call(
        dense_kernel,
        grid_spec=pltpu.PrefetchScalarGridSpec(
            num_scalar_prefetch=1,
            grid=(1,),
            in_specs=[
                pl.BlockSpec(memory_space=pl.ANY),
                whole(locals_, rows, width),
                whole(width, hid),
                whole(locals_, rows, hid),
            ],
            out_specs=[
                whole(locals_, rows, hid),
                whole(width, hid),
                whole(locals_, rows, width),
                pl.BlockSpec(memory_space=pl.ANY),
            ],
            scratch_shapes=[
                pltpu.VMEM((locals_, rows, width), jnp.float32),
                pltpu.VMEM((peers, rows, width), returned.dtype),
                pltpu.SemaphoreType.DMA((peers,)),
            ],
        ),
        out_shape=[
            jax.ShapeDtypeStruct((locals_, rows, hid), jnp.bfloat16),
            jax.ShapeDtypeStruct((width, hid), jnp.float32),
            jax.ShapeDtypeStruct((locals_, rows, width), jnp.bfloat16),
            jax.ShapeDtypeStruct((peers, rows, width), jnp.bfloat16),
        ],
        compiler_params=params(),
    )(asked, returned, start, weight, cotangent)


def finish_kernel(asked_ref, returned_ref, start_ref, out_ref, total_ref, landed_ref, sems):
    add_returned(asked_ref, returned_ref, start_ref, total_ref, landed_ref, sems)
    out_ref[...] = total_ref[...].astype(out_ref.dtype)


def finish(asked, returned, start):
    peers, rows, width = returned.shape
    locals_ = start.shape[0]
    return pl.pallas_call(
        finish_kernel,
        grid_spec=pltpu.PrefetchScalarGridSpec(
            num_scalar_prefetch=1,
            grid=(1,),
            in_specs=[pl.BlockSpec(memory_space=pl.ANY), whole(locals_, rows, width)],
            out_specs=whole(locals_, rows, width),
            scratch_shapes=[
                pltpu.VMEM((locals_, rows, width), jnp.float32),
                pltpu.VMEM((peers, rows, width), returned.dtype),
                pltpu.SemaphoreType.DMA((peers,)),
            ],
        ),
        out_shape=jax.ShapeDtypeStruct((locals_, rows, width), jnp.bfloat16),
        compiler_params=params(),
    )(asked, returned, start)


def exchange(values):
    return lax.all_to_all(values, "nodes", split_axis=0, concat_axis=0, tiled=True)


ASKED, VIA, RELAYED, CAME_VIA, WANTED, FITS = range(6)
OPEN = -2


def plan_kernel(
    me_ref, wanted_ref, blocks_ref, plan_ref, out_ref, free_ref, rows_ref, columns_ref, known_ref, sems
):
    peers = wanted_ref.shape[0]
    groups = peers // 8
    me = me_ref[0]
    raw = wanted_ref[...]
    u_ids = lax.broadcasted_iota(jnp.int32, raw.shape, 0)
    named = (raw >= 0).astype(jnp.float32)
    flipped = named.T
    skewed = flipped
    for bit in range(peers.bit_length() - 1):
        turned = pltpu.roll(skewed, peers - (1 << bit), 1)
        skewed = jnp.where(((u_ids >> bit) & 1) == 1, turned, skewed)
    free = (1.0 - skewed.T).astype(jnp.int32)
    free_ref[...] = jnp.broadcast_to(free[:, None, :], free_ref.shape)
    route = jnp.where((named > 0) & (flipped > 0), OPEN, -1)
    spare = 1 - flipped.astype(jnp.int32)
    at_ids = lax.broadcasted_iota(jnp.int32, (8, peers), 0)
    v_ids = lax.broadcasted_iota(jnp.int32, (8, peers), 1)

    def left_open(routes):
        count = (routes[0] == OPEN).astype(jnp.float32)
        for part in routes[1:]:
            count += (part == OPEN).astype(jnp.float32)
        return jnp.sum(count).astype(jnp.int32)

    def one(turn, routes, spares):
        shifts = [(turn + 8 * group) & (peers - 1) for group in range(groups)]
        rooms = [free_ref[shift] for shift in shifts]
        next_routes, next_spares, taken = [], [], []
        for route, spare, shift, room in zip(routes, spares, shifts, rooms):
            fits = (route == OPEN) & ((spare & room) > 0)
            first = jnp.min(jnp.where(fits, at_ids, 8), axis=0, keepdims=True)
            chosen = fits & (at_ids == first)
            taken.append(jnp.where(first < 8, 0, room))
            next_routes.append(jnp.where(chosen, (v_ids + shift) & (peers - 1), route))
            next_spares.append(pltpu.roll(jnp.where(chosen, 0, spare), peers - 1, 1))
        for shift, room in zip(shifts, taken):
            free_ref[shift] = room
        return tuple(next_routes), tuple(next_spares)

    def some(carry):
        turn, _, routes, spares = carry
        for ahead in range(TURNS):
            routes, spares = one(turn + ahead, routes, spares)
        return turn + TURNS, left_open(routes), routes, spares

    routes = tuple(route[8 * group : 8 * group + 8] for group in range(groups))
    spares = tuple(
        pltpu.roll(spare[8 * group : 8 * group + 8], (peers - 8 * group) % peers, 1)
        for group in range(groups)
    )
    _, left, routes, _ = lax.while_loop(
        lambda carry: (carry[0] < peers) & (carry[1] > 0),
        some,
        (jnp.int32(0), left_open(routes), routes, spares),
    )
    route = jnp.concatenate(routes, 0)
    rows_ref[...] = route
    columns_ref[...] = route.astype(jnp.float32).T.astype(jnp.int32)
    plan_ref[VIA : VIA + 1, :] = rows_ref[pl.ds(me, 1), :]
    plan_ref[CAME_VIA : CAME_VIA + 1, :] = columns_ref[pl.ds(me, 1), :]
    plan_ref[RELAYED : RELAYED + 1, :] = jnp.max(
        jnp.where(route == me, u_ids, -1), axis=0, keepdims=True
    )
    columns_ref[...] = raw.astype(jnp.float32).T.astype(jnp.int32)
    plan_ref[ASKED : ASKED + 1, :] = columns_ref[pl.ds(me, 1), :]
    plan_ref[WANTED : WANTED + 1, :] = wanted_ref[pl.ds(me, 1), :]
    twice = jnp.sum((raw >= TWICE).astype(jnp.float32)).astype(jnp.int32)
    fits = jnp.where((left == 0) & (twice == 0), 1, 0)
    plan_ref[FITS:, :] = jnp.full((plan_ref.shape[0] - FITS, peers), fits, jnp.int32)
    tell = pltpu.make_async_copy(plan_ref, known_ref, sems.at[2 * peers])
    tell.start()
    tell.wait()

    @pl.when(fits > 0)
    def _():
        send_first(known_ref, blocks_ref, out_ref, sems)


def make_plan(myself, wanted, blocks):
    peers = wanted.shape[0]
    locals_, rows, width = blocks.shape
    square = pltpu.VMEM((peers, peers), jnp.int32)
    return pl.pallas_call(
        plan_kernel,
        grid_spec=pltpu.PrefetchScalarGridSpec(
            num_scalar_prefetch=1,
            grid=(1,),
            in_specs=[whole(peers, peers), whole(locals_, rows, width)],
            out_specs=[whole(8, peers), pl.BlockSpec(memory_space=pl.ANY)],
            scratch_shapes=[
                pltpu.VMEM((peers, 8, peers), jnp.int32),
                square,
                square,
                pltpu.SMEM((8, peers), jnp.int32),
                pltpu.SemaphoreType.DMA((2 * peers + 1,)),
            ],
        ),
        out_shape=[
            jax.ShapeDtypeStruct((8, peers), jnp.int32),
            jax.ShapeDtypeStruct((peers, rows // 2, width), blocks.dtype),
        ],
        compiler_params=params(),
    )(jnp.full((1,), myself, jnp.int32), wanted, blocks)


def each_peer(peers, act):
    def step(q, carry):
        act(q)
        return carry

    lax.fori_loop(0, peers, step, 0, unroll=8)


def send_first(plan_ref, blocks_ref, out_ref, sems):
    peers = plan_ref.shape[1]
    half = blocks_ref.shape[1] // 2

    def direct(q):
        block = jnp.maximum(plan_ref[ASKED, q], 0)
        return pltpu.make_async_copy(
            blocks_ref.at[block, pl.ds(0, half)], out_ref.at[q, pl.ds(0, half)], sems.at[q]
        )

    def relayed(q):
        block = jnp.maximum(plan_ref[ASKED, q], 0)
        via = jnp.maximum(plan_ref[VIA, q], 0)
        return pltpu.make_async_copy(
            blocks_ref.at[block, pl.ds(half, half)],
            out_ref.at[via, pl.ds(0, half)],
            sems.at[peers + q],
        )

    def start(q):
        @pl.when(plan_ref[ASKED, q] >= 0)
        def _():
            direct(q).start()

        @pl.when(plan_ref[VIA, q] >= 0)
        def _():
            relayed(q).start()

    def wait(q):
        @pl.when(plan_ref[ASKED, q] >= 0)
        def _():
            direct(q).wait()

        @pl.when(plan_ref[VIA, q] >= 0)
        def _():
            relayed(q).wait()

    each_peer(peers, start)
    each_peer(peers, wait)


def tiles_spec(rows):
    return pl.BlockSpec(
        (GROUP, rows, rows), lambda i, plan, slots: (jnp.minimum(i, slots[3, 0]), 0, 0)
    )


ROW, HOME, COLUMN, LAST = range(4)


def products_kernel(plan_ref, slots_ref, blocks_ref, tiles_ref, out_ref, total_ref):
    step = pl.program_id(0)
    peers = plan_ref.shape[1]
    rows = blocks_ref.shape[1]
    half = rows // 2
    locals_ = blocks_ref.shape[0]

    @pl.when(step == 0)
    def _():
        total_ref[...] = jnp.zeros_like(total_ref)

        def second_half(q):
            @pl.when((plan_ref[ASKED, q] >= 0) & (plan_ref[WANTED, q] < 0))
            def _():
                out_ref[q, pl.ds(0, half)] = blocks_ref[plan_ref[ASKED, q], pl.ds(half, half)]

        each_peer(peers, second_half)

    @pl.when(step <= slots_ref[LAST, 0])
    def _():
        for at in range(GROUP):
            slot = step * GROUP + at
            row, home, column = slots_ref[ROW, slot], slots_ref[HOME, slot], slots_ref[COLUMN, slot]
            tile = tiles_ref[at]
            product = lax.dot_general(
                tile, blocks_ref[row], (((0,), (0,)), ((), ())), preferred_element_type=jnp.float32
            )
            out_ref[home, pl.ds(0, rows)] = product.astype(out_ref.dtype)

            @pl.when(column < locals_)
            def _():
                total_ref[column] += product
                total_ref[row] += jnp.dot(
                    tile, blocks_ref[column], preferred_element_type=jnp.float32
                )


def own_products(plan, slots, blocks, tile_values, extra):
    peers = plan.shape[1]
    slot_total, rows, _ = tile_values.shape
    locals_, _, width = blocks.shape
    return pl.pallas_call(
        products_kernel,
        grid_spec=pltpu.PrefetchScalarGridSpec(
            num_scalar_prefetch=2,
            grid=(slot_total // GROUP,),
            in_specs=[whole(locals_, rows, width), tiles_spec(rows)],
            out_specs=[whole(peers, rows + extra, width), whole(locals_, rows, width)],
        ),
        out_shape=[
            jax.ShapeDtypeStruct((peers, rows + extra, width), blocks.dtype),
            jax.ShapeDtypeStruct((locals_, rows, width), jnp.float32),
        ],
        compiler_params=params(),
        cost_estimate=pl.CostEstimate(
            flops=3 * slot_total * rows * rows * width, bytes_accessed=24 << 20, transcendentals=0
        ),
    )(plan, slots, blocks, tile_values)


def three_parts(value):
    high = value.astype(jnp.bfloat16)
    rest = value - high.astype(jnp.float32)
    middle = rest.astype(jnp.bfloat16)
    low = (rest - middle.astype(jnp.float32)).astype(jnp.bfloat16)
    return [part.astype(jnp.float32) for part in (high, middle, low)]


def relay_kernel(plan_ref, came_ref, _, out_ref, held_ref, sems, *grad_refs):
    peers = plan_ref.shape[1]
    half = came_ref.shape[1] - (EXTRA if grad_refs else 0)

    def take(q):
        source = jnp.maximum(plan_ref[RELAYED, q], 0)
        return pltpu.make_async_copy(
            came_ref.at[source, pl.ds(0, half)], held_ref.at[q], sems.at[q]
        )

    def give(q):
        return pltpu.make_async_copy(
            held_ref.at[q], out_ref.at[q, pl.ds(half, half)], sems.at[peers + q]
        )

    def start(q):
        @pl.when(plan_ref[RELAYED, q] >= 0)
        def _():
            take(q).start()

    def turn(q):
        @pl.when(plan_ref[RELAYED, q] >= 0)
        def _():
            take(q).wait()
            give(q).start()

    def wait(q):
        @pl.when(plan_ref[RELAYED, q] >= 0)
        def _():
            give(q).wait()

    if grad_refs:
        (staged_ref,) = grad_refs
        bring = pltpu.make_async_copy(
            came_ref.at[:, pl.ds(half, EXTRA)], staged_ref, sems.at[2 * peers]
        )
        bring.start()
    each_peer(peers, start)
    if grad_refs:
        bring.wait()
        sums = jnp.sum(staged_ref[...].astype(jnp.float32), axis=0)
        own = (sums[4:6] + sums[2:4]) + sums[0:2]
        parts = three_parts(own)
        packed = jnp.concatenate(parts + [jnp.zeros((EXTRA - 6, own.shape[1]), jnp.float32)], 0)
        staged_ref[...] = jnp.broadcast_to(packed[None], staged_ref.shape).astype(jnp.bfloat16)
        put = pltpu.make_async_copy(
            staged_ref, out_ref.at[:, pl.ds(2 * half, EXTRA)], sems.at[2 * peers + 1]
        )
        put.start()
    each_peer(peers, turn)
    if grad_refs:
        put.wait()
    each_peer(peers, wait)


def relay(plan, came, outgoing, with_grad):
    peers, _, width = came.shape
    scratch = [
        pltpu.VMEM((peers, came.shape[1] - (EXTRA if with_grad else 0), width), came.dtype),
        pltpu.SemaphoreType.DMA((2 * peers + 2,)),
    ]
    if with_grad:
        scratch.append(pltpu.VMEM((peers, EXTRA, width), jnp.bfloat16))
    anywhere = pl.BlockSpec(memory_space=pl.ANY)
    return pl.pallas_call(
        relay_kernel,
        grid_spec=pltpu.PrefetchScalarGridSpec(
            num_scalar_prefetch=1,
            grid=(1,),
            in_specs=[anywhere, anywhere],
            out_specs=anywhere,
            scratch_shapes=scratch,
        ),
        out_shape=jax.ShapeDtypeStruct(outgoing.shape, outgoing.dtype),
        input_output_aliases={2: 0},
        compiler_params=params(),
    )(plan, came, outgoing)


def early_kernel(plan_ref, slots_ref, first_ref, tiles_ref, start_ref, total_ref, sums_ref):
    step = pl.program_id(0)
    half = tiles_ref.shape[2]
    locals_ = start_ref.shape[0]

    @pl.when(step == 0)
    def _():
        sums_ref[pl.ds(0, locals_)] = start_ref[...]

    @pl.when(step <= slots_ref[LAST, 0])
    def _():
        for at in range(GROUP):
            slot = step * GROUP + at
            remote = slots_ref[COLUMN, slot] == locals_
            row = jnp.where(remote, slots_ref[ROW, slot], locals_)
            sums_ref[row] += jnp.dot(
                tiles_ref[at],
                first_ref[slots_ref[HOME, slot], pl.ds(0, half)],
                preferred_element_type=jnp.float32,
            )

    @pl.when(step == pl.num_programs(0) - 1)
    def _():
        total_ref[...] = sums_ref[pl.ds(0, locals_)]


def early_products(plan, slots, first, tile_values, start):
    slot_total, rows, _ = tile_values.shape
    locals_, _, width = start.shape
    return pl.pallas_call(
        early_kernel,
        grid_spec=pltpu.PrefetchScalarGridSpec(
            num_scalar_prefetch=2,
            grid=(slot_total // GROUP,),
            in_specs=[
                whole(*first.shape),
                pl.BlockSpec(
                    (GROUP, rows, rows // 2),
                    lambda i, plan, slots: (jnp.minimum(i, slots[LAST, 0]), 0, 0),
                ),
                whole(*start.shape),
            ],
            out_specs=whole(*start.shape),
            scratch_shapes=[pltpu.VMEM((locals_ + 1, rows, width), jnp.float32)],
        ),
        out_shape=jax.ShapeDtypeStruct(start.shape, start.dtype),
        compiler_params=params(),
        cost_estimate=pl.CostEstimate(
            flops=slot_total * rows * rows * width, bytes_accessed=12 << 20, transcendentals=0
        ),
    )(plan, slots, first, tile_values, start)


def late_scratch(second, tile_values, start):
    peers, _, width = second.shape
    slot_total, rows, _ = tile_values.shape
    return [
        pltpu.VMEM((start.shape[0] + 1, rows, width), jnp.float32),
        pltpu.VMEM(second.shape, second.dtype),
        pltpu.VMEM((slot_total, rows, rows // 2), tile_values.dtype),
        pltpu.SemaphoreType.DMA((PARTS + slot_total // GROUP,)),
    ]


def late_sums(plan_ref, slots_ref, second_ref, tiles_ref, start_ref, total_ref, landed_ref, held_ref, sems):
    peers = plan_ref.shape[1]
    slot_total, rows, half = held_ref.shape
    locals_ = start_ref.shape[0]
    share = peers // PARTS

    def landing(part):
        piece = pl.ds(part * share, share)
        return pltpu.make_async_copy(second_ref.at[piece], landed_ref.at[piece], sems.at[part])

    def holding(group):
        piece = pl.ds(group * GROUP, GROUP)
        return pltpu.make_async_copy(
            tiles_ref.at[piece, :, pl.ds(half, half)], held_ref.at[piece], sems.at[PARTS + group]
        )

    for part in range(PARTS):
        landing(part).start()
    groups = slot_total // GROUP
    for group in range(groups):

        @pl.when(group <= slots_ref[LAST, 0])
        def _():
            holding(group).start()

    total_ref[pl.ds(0, locals_)] = start_ref[...]

    def add(q, carry):
        block = plan_ref[ASKED, q]

        @pl.when(block >= 0)
        def _():
            total_ref[block] += landed_ref[q, pl.ds(0, rows)].astype(jnp.float32)

        return carry

    for part in range(PARTS):
        landing(part).wait()
        lax.fori_loop(part * share, (part + 1) * share, add, 0, unroll=4)

    def multiply(group, carry):
        @pl.when(group <= slots_ref[LAST, 0])
        def _():
            holding(group).wait()
            for at in range(GROUP):
                slot = group * GROUP + at
                home = slots_ref[HOME, slot]
                remote = slots_ref[COLUMN, slot] == locals_
                row = jnp.where(remote, slots_ref[ROW, slot], locals_)
                via = plan_ref[CAME_VIA, home]
                source = jnp.where(via >= 0, via, home)
                offset = pl.multiple_of(jnp.where(via >= 0, half, 0), half)
                total_ref[row] += jnp.dot(
                    held_ref[slot],
                    landed_ref[source, pl.ds(offset, half)],
                    preferred_element_type=jnp.float32,
                )

        return carry

    lax.fori_loop(0, groups, multiply, 0)


def layer_kernel(
    plan_ref,
    slots_ref,
    second_ref,
    tiles_ref,
    start_ref,
    weight_ref,
    cotangent_ref,
    hidden_ref,
    upstream_ref,
    out_ref,
    total_ref,
    landed_ref,
    held_ref,
    late_sems,
    grad_ref,
    rows_ref,
    staged_ref,
    sems,
):
    late_sums(
        plan_ref,
        slots_ref,
        second_ref,
        tiles_ref,
        start_ref,
        total_ref,
        landed_ref,
        held_ref,
        late_sems,
    )
    peers = plan_ref.shape[1]
    half = held_ref.shape[2]
    width = upstream_ref.shape[2]
    weight = weight_ref[...]
    grad_ref[...] = jnp.zeros_like(grad_ref)

    def block_step(k, carry):
        aggregated = total_ref[k].astype(jnp.bfloat16)
        preact = jnp.dot(aggregated, weight, preferred_element_type=jnp.float32)
        sigma = 1.0 / (1.0 + jnp.exp(-preact))
        hidden_ref[k] = (preact * sigma).astype(jnp.bfloat16)
        delta = (
            cotangent_ref[k].astype(jnp.float32) * sigma * (1.0 + preact * (1.0 - sigma))
        ).astype(jnp.bfloat16)
        grad_ref[...] += lax.dot_general(
            aggregated, delta, (((0,), (0,)), ((), ())), preferred_element_type=jnp.float32
        )
        upstream_ref[k] = lax.dot_general(
            delta, weight, (((1,), (1,)), ((), ())), preferred_element_type=jnp.float32
        ).astype(jnp.bfloat16)
        return carry

    lax.fori_loop(0, cotangent_ref.shape[0], block_step, 0, unroll=2)
    for side in range(2):
        parts = three_parts(grad_ref[:, side * width : (side + 1) * width])
        for at, part in enumerate(parts):
            rows_ref[:, 2 * at + side, :] = part
    for at in range(6, EXTRA):
        rows_ref[:, at, :] = jnp.zeros((peers, width), jnp.float32)
    staged_ref[...] = rows_ref[...].astype(jnp.bfloat16)
    put = pltpu.make_async_copy(staged_ref, out_ref.at[:, pl.ds(half, EXTRA)], sems.at[2 * peers])
    put.start()
    send_first(plan_ref, upstream_ref, out_ref, sems)
    put.wait()


def layer(plan, slots, second, tile_values, start, weight, cotangent):
    peers, _, width = second.shape
    _, rows, _ = tile_values.shape
    locals_ = start.shape[0]
    hid = weight.shape[1]
    assert width == peers and hid == 2 * width
    anywhere = pl.BlockSpec(memory_space=pl.ANY)
    return pl.pallas_call(
        layer_kernel,
        grid_spec=pltpu.PrefetchScalarGridSpec(
            num_scalar_prefetch=2,
            grid=(1,),
            in_specs=[
                anywhere,
                anywhere,
                whole(*start.shape),
                whole(width, hid),
                whole(locals_, rows, hid),
            ],
            out_specs=[whole(locals_, rows, hid), whole(locals_, rows, width), anywhere],
            scratch_shapes=late_scratch(second, tile_values, start)
            + [
                pltpu.VMEM((width, hid), jnp.float32),
                pltpu.VMEM((peers, EXTRA, width), jnp.float32),
                pltpu.VMEM((peers, EXTRA, width), jnp.bfloat16),
                pltpu.SemaphoreType.DMA((2 * peers + 1,)),
            ],
        ),
        out_shape=[
            jax.ShapeDtypeStruct((locals_, rows, hid), jnp.bfloat16),
            jax.ShapeDtypeStruct((locals_, rows, width), jnp.bfloat16),
            jax.ShapeDtypeStruct((peers, rows // 2 + EXTRA, width), jnp.bfloat16),
        ],
        compiler_params=params(),
    )(plan, slots, second, tile_values, start, weight, cotangent)


def last_kernel(
    scale,
    plan_ref,
    slots_ref,
    second_ref,
    tiles_ref,
    start_ref,
    out_ref,
    weight_grad_ref,
    total_ref,
    landed_ref,
    held_ref,
    late_sems,
    rows_ref,
):
    late_sums(
        plan_ref,
        slots_ref,
        second_ref,
        tiles_ref,
        start_ref,
        total_ref,
        landed_ref,
        held_ref,
        late_sems,
    )
    rows = held_ref.shape[1]
    width = out_ref.shape[2]
    out_ref[...] = total_ref[pl.ds(0, out_ref.shape[0])].astype(out_ref.dtype)
    rows_ref[...] = landed_ref[:, pl.ds(rows, EXTRA)].astype(jnp.float32)
    for side in range(2):
        weight_grad_ref[:, side * width : (side + 1) * width] = (
            rows_ref[:, 4 + side, :] + rows_ref[:, 2 + side, :] + rows_ref[:, side, :]
        ) * scale


def last(plan, slots, second, tile_values, start, scale):
    peers, _, width = second.shape
    _, rows, _ = tile_values.shape
    locals_ = start.shape[0]
    anywhere = pl.BlockSpec(memory_space=pl.ANY)
    return pl.pallas_call(
        functools.partial(last_kernel, scale),
        grid_spec=pltpu.PrefetchScalarGridSpec(
            num_scalar_prefetch=2,
            grid=(1,),
            in_specs=[anywhere, anywhere, whole(*start.shape)],
            out_specs=[whole(locals_, rows, width), whole(peers, 2 * width)],
            scratch_shapes=late_scratch(second, tile_values, start)
            + [pltpu.VMEM((peers, EXTRA, width), jnp.float32)],
        ),
        out_shape=[
            jax.ShapeDtypeStruct((locals_, rows, width), jnp.bfloat16),
            jax.ShapeDtypeStruct((peers, 2 * width), jnp.float32),
        ],
        compiler_params=params(),
    )(plan, slots, second, tile_values, start)


def on_device(features, weight, cotangent, block_pairs, tile_counts, tile_values):
    peers = lax.axis_size("nodes")
    myself = lax.axis_index("nodes")
    rows = tile_values.shape[1]
    width = features.shape[1]
    hid = weight.shape[1]
    locals_ = features.shape[0] // rows
    count = tile_counts[0]
    slot_ids = jnp.arange(block_pairs.shape[0], dtype=jnp.int32)
    peer_ids = jnp.arange(peers, dtype=jnp.int32)
    row_local = jnp.clip(block_pairs[:, 0] - myself * locals_, 0, locals_ - 1)
    col_blocks = block_pairs[:, 1]
    home = col_blocks // locals_
    column = col_blocks % locals_
    live = slot_ids < count
    remote = live & (home != myself)
    hit = (home[None, :] == peer_ids[:, None]) & remote[None, :]
    wanted = jnp.max(jnp.where(hit, column[None, :], -1), axis=1)
    named_twice = jnp.sum(hit.astype(jnp.int32), axis=1) > 1
    wanted = wanted + jnp.where(named_twice, TWICE, 0)
    everyones = exchange(jnp.broadcast_to(wanted[None, :], (peers, peers)))
    blocks = features.reshape(locals_, rows, width)
    plan, sending = make_plan(myself, everyones, blocks)
    cotangent_blocks = cotangent.reshape(locals_, rows, hid)
    scale = 1.0 / math.sqrt(peers * locals_ * rows)

    def sparse():
        slots = jnp.stack(
            [
                row_local,
                jnp.where(remote, home, myself),
                jnp.where(live & ~remote, column, jnp.where(remote, locals_, locals_ + 1)),
                jnp.broadcast_to((count - 1) // GROUP, row_local.shape),
            ]
        )
        first = exchange(sending)
        outgoing, total = own_products(plan, slots, blocks, tile_values, 0)
        first, outgoing = lax.optimization_barrier((first, outgoing))
        second = exchange(relay(plan, first, outgoing, False))
        total = early_products(plan, slots, first, tile_values, total)
        hidden, upstream, halves = layer(
            plan, slots, second, tile_values, total, weight, cotangent_blocks
        )
        first = exchange(halves)
        outgoing, total = own_products(plan, slots, upstream, tile_values, EXTRA)
        first, outgoing = lax.optimization_barrier((first, outgoing))
        second = exchange(relay(plan, first, outgoing, True))
        total = early_products(plan, slots, first, tile_values, total)
        feature_grad, weight_grad = last(plan, slots, second, tile_values, total, scale)
        return hidden, weight_grad, feature_grad

    def full():
        asked = plan[ASKED]
        asked = jnp.where(asked >= 0, asked % TWICE, -1)
        dest = jnp.where(live, jnp.where(remote, home, peers + column), -1)
        earlier = (home[None, :] == home[:, None]) & (slot_ids[None, :] < slot_ids[:, None])
        again = jnp.any(earlier, axis=1).astype(jnp.int32)
        arrived = exchange(pick(asked, blocks))
        outgoing, total = transposed_products(row_local, dest, again, blocks, tile_values, peers)
        returned = exchange(outgoing)
        total = direct_products(row_local, dest, arrived, tile_values, total)
        hidden, local_grad, upstream, requested = dense(
            asked, returned, total, weight, cotangent_blocks
        )
        row_sum = jnp.sum(exchange(local_grad), axis=0) * scale
        weight_grad = exchange(jnp.broadcast_to(row_sum, local_grad.shape))
        arrived = exchange(requested)
        outgoing, total = transposed_products(row_local, dest, again, upstream, tile_values, peers)
        returned = exchange(outgoing)
        total = direct_products(row_local, dest, arrived, tile_values, total)
        return hidden, weight_grad, finish(asked, returned, total)

    hidden, weight_grad, feature_grad = lax.cond(plan[FITS, 0] > 0, sparse, full)
    return (
        hidden.reshape(locals_ * rows, hid),
        weight_grad,
        feature_grad.reshape(locals_ * rows, width),
    )


def solution(mesh):
    return jax.shard_map(
        on_device,
        mesh=mesh,
        in_specs=(
            P("nodes", None),
            P(),
            P("nodes", None),
            P("nodes", None),
            P("nodes"),
            P("nodes", None, None),
        ),
        out_specs=(P("nodes", None), P(), P("nodes", None)),
        check_vma=False,
    )
```

```python
import functools
import math

import jax
import jax.numpy as jnp
from jax import lax
from jax.experimental import pallas as pl
from jax.experimental.pallas import tpu as pltpu
from jax.sharding import PartitionSpec as P

VMEM_LIMIT = 60 * 1024 * 1024
GROUP = 16
PARTS = 4
EXTRA = 16
TWICE = 64
TURNS = 8


def whole(*shape):
    return pl.BlockSpec(shape, lambda *_: (0,) * len(shape), pipeline_mode=pl.Buffered(1))


def params(limit=VMEM_LIMIT):
    return pltpu.CompilerParams(vmem_limit_bytes=limit)


def send_blocks(asked_ref, blocks_ref, out_ref, sems):
    def copy(q):
        block = jnp.maximum(asked_ref[q], 0)
        return pltpu.make_async_copy(blocks_ref.at[block], out_ref.at[q], sems.at[q])

    def start(q, carry):
        @pl.when(asked_ref[q] >= 0)
        def _():
            copy(q).start()

        return carry

    def wait(q, carry):
        @pl.when(asked_ref[q] >= 0)
        def _():
            copy(q).wait()

        return carry

    peers = asked_ref.shape[0]
    lax.fori_loop(0, peers, start, 0)
    lax.fori_loop(0, peers, wait, 0)


def pick(asked, blocks):
    peers = asked.shape[0]
    locals_, rows, width = blocks.shape
    return pl.pallas_call(
        send_blocks,
        grid_spec=pltpu.PrefetchScalarGridSpec(
            num_scalar_prefetch=1,
            grid=(1,),
            in_specs=[whole(locals_, rows, width)],
            out_specs=pl.BlockSpec(memory_space=pl.ANY),
            scratch_shapes=[pltpu.SemaphoreType.DMA((peers,))],
        ),
        out_shape=jax.ShapeDtypeStruct((peers, rows, width), blocks.dtype),
        compiler_params=params(),
    )(asked, blocks)


def transposed_kernel(
    peers, row_ref, dest_ref, again_ref, blocks_ref, tiles_ref, out_ref, total_ref
):
    step = pl.program_id(0)

    @pl.when(step == 0)
    def _():
        total_ref[...] = jnp.zeros_like(total_ref)

    def visit(at, carry):
        slot = step * GROUP + at
        dest = dest_ref[slot]

        @pl.when(dest >= 0)
        def _():
            row = row_ref[slot]
            product = lax.dot_general(
                tiles_ref[at],
                blocks_ref[row],
                (((0,), (0,)), ((), ())),
                preferred_element_type=jnp.float32,
            )
            remote = dest < peers

            @pl.when(remote & (again_ref[slot] == 0))
            def _():
                out_ref[dest] = product.astype(out_ref.dtype)

            @pl.when(remote & (again_ref[slot] == 1))
            def _():
                out_ref[dest] = (out_ref[dest].astype(jnp.float32) + product).astype(out_ref.dtype)

            @pl.when(jnp.logical_not(remote))
            def _():
                column = dest - peers
                total_ref[column] += product
                total_ref[row] += jnp.dot(
                    tiles_ref[at], blocks_ref[column], preferred_element_type=jnp.float32
                )

        return carry

    lax.fori_loop(0, GROUP, visit, 0)


def transposed_products(row_local, dest, again, blocks, tile_values, peers):
    slots, rows, _ = tile_values.shape
    locals_, _, width = blocks.shape
    return pl.pallas_call(
        functools.partial(transposed_kernel, peers),
        grid_spec=pltpu.PrefetchScalarGridSpec(
            num_scalar_prefetch=3,
            grid=(slots // GROUP,),
            in_specs=[
                whole(locals_, rows, width),
                pl.BlockSpec((GROUP, rows, rows), lambda i, *_: (i, 0, 0)),
            ],
            out_specs=[whole(peers, rows, width), whole(locals_, rows, width)],
        ),
        out_shape=[
            jax.ShapeDtypeStruct((peers, rows, width), blocks.dtype),
            jax.ShapeDtypeStruct((locals_, rows, width), jnp.float32),
        ],
        compiler_params=params(),
        cost_estimate=pl.CostEstimate(
            flops=3 * slots * rows * rows * width, bytes_accessed=24 << 20, transcendentals=0
        ),
    )(row_local, dest, again, blocks, tile_values)


def direct_kernel(peers, row_ref, dest_ref, arrived_ref, tiles_ref, start_ref, total_ref):
    step = pl.program_id(0)

    @pl.when(step == 0)
    def _():
        total_ref[...] = start_ref[...]

    def visit(at, carry):
        slot = step * GROUP + at
        source = dest_ref[slot]

        @pl.when((source >= 0) & (source < peers))
        def _():
            total_ref[row_ref[slot]] += jnp.dot(
                tiles_ref[at], arrived_ref[source], preferred_element_type=jnp.float32
            )

        return carry

    lax.fori_loop(0, GROUP, visit, 0)


def direct_products(row_local, dest, arrived, tile_values, start):
    slots, rows, _ = tile_values.shape
    peers, _, width = arrived.shape
    locals_ = start.shape[0]
    return pl.pallas_call(
        functools.partial(direct_kernel, peers),
        grid_spec=pltpu.PrefetchScalarGridSpec(
            num_scalar_prefetch=2,
            grid=(slots // GROUP,),
            in_specs=[
                whole(peers, rows, width),
                pl.BlockSpec((GROUP, rows, rows), lambda i, *_: (i, 0, 0)),
                whole(locals_, rows, width),
            ],
            out_specs=whole(locals_, rows, width),
        ),
        out_shape=jax.ShapeDtypeStruct((locals_, rows, width), jnp.float32),
        compiler_params=params(),
        cost_estimate=pl.CostEstimate(
            flops=2 * slots * rows * rows * width, bytes_accessed=24 << 20, transcendentals=0
        ),
    )(row_local, dest, arrived, tile_values, start)


def add_returned(asked_ref, returned_ref, start_ref, total_ref, landed_ref, sems):
    def copy(q):
        return pltpu.make_async_copy(returned_ref.at[q], landed_ref.at[q], sems.at[q])

    def start(q, carry):
        @pl.when(asked_ref[q] >= 0)
        def _():
            copy(q).start()

        return carry

    def add(q, carry):
        block = asked_ref[q]

        @pl.when(block >= 0)
        def _():
            copy(q).wait()
            total_ref[block] += landed_ref[q].astype(jnp.float32)

        return carry

    peers = asked_ref.shape[0]
    lax.fori_loop(0, peers, start, 0)
    total_ref[...] = start_ref[...]
    lax.fori_loop(0, peers, add, 0)


def dense_kernel(
    asked_ref,
    returned_ref,
    start_ref,
    weight_ref,
    cotangent_ref,
    hidden_ref,
    grad_ref,
    upstream_ref,
    out_ref,
    total_ref,
    landed_ref,
    sems,
):
    add_returned(asked_ref, returned_ref, start_ref, total_ref, landed_ref, sems)
    grad_ref[...] = jnp.zeros_like(grad_ref)
    weight = weight_ref[...]

    def block_step(k, carry):
        aggregated = total_ref[k].astype(jnp.bfloat16)
        preact = jnp.dot(aggregated, weight, preferred_element_type=jnp.float32)
        sigma = 1.0 / (1.0 + jnp.exp(-preact))
        hidden_ref[k] = (preact * sigma).astype(jnp.bfloat16)
        delta = (
            cotangent_ref[k].astype(jnp.float32) * sigma * (1.0 + preact * (1.0 - sigma))
        ).astype(jnp.bfloat16)
        grad_ref[...] += lax.dot_general(
            aggregated, delta, (((0,), (0,)), ((), ())), preferred_element_type=jnp.float32
        )
        upstream_ref[k] = lax.dot_general(
            delta, weight, (((1,), (1,)), ((), ())), preferred_element_type=jnp.float32
        ).astype(jnp.bfloat16)
        return carry

    lax.fori_loop(0, total_ref.shape[0], block_step, 0)
    send_blocks(asked_ref, upstream_ref, out_ref, sems)


def dense(asked, returned, start, weight, cotangent):
    peers, rows, width = returned.shape
    locals_ = start.shape[0]
    hid = weight.shape[1]
    return pl.pallas_call(
        dense_kernel,
        grid_spec=pltpu.PrefetchScalarGridSpec(
            num_scalar_prefetch=1,
            grid=(1,),
            in_specs=[
                pl.BlockSpec(memory_space=pl.ANY),
                whole(locals_, rows, width),
                whole(width, hid),
                whole(locals_, rows, hid),
            ],
            out_specs=[
                whole(locals_, rows, hid),
                whole(width, hid),
                whole(locals_, rows, width),
                pl.BlockSpec(memory_space=pl.ANY),
            ],
            scratch_shapes=[
                pltpu.VMEM((locals_, rows, width), jnp.float32),
                pltpu.VMEM((peers, rows, width), returned.dtype),
                pltpu.SemaphoreType.DMA((peers,)),
            ],
        ),
        out_shape=[
            jax.ShapeDtypeStruct((locals_, rows, hid), jnp.bfloat16),
            jax.ShapeDtypeStruct((width, hid), jnp.float32),
            jax.ShapeDtypeStruct((locals_, rows, width), jnp.bfloat16),
            jax.ShapeDtypeStruct((peers, rows, width), jnp.bfloat16),
        ],
        compiler_params=params(),
    )(asked, returned, start, weight, cotangent)


def finish_kernel(asked_ref, returned_ref, start_ref, out_ref, total_ref, landed_ref, sems):
    add_returned(asked_ref, returned_ref, start_ref, total_ref, landed_ref, sems)
    out_ref[...] = total_ref[...].astype(out_ref.dtype)


def finish(asked, returned, start):
    peers, rows, width = returned.shape
    locals_ = start.shape[0]
    return pl.pallas_call(
        finish_kernel,
        grid_spec=pltpu.PrefetchScalarGridSpec(
            num_scalar_prefetch=1,
            grid=(1,),
            in_specs=[pl.BlockSpec(memory_space=pl.ANY), whole(locals_, rows, width)],
            out_specs=whole(locals_, rows, width),
            scratch_shapes=[
                pltpu.VMEM((locals_, rows, width), jnp.float32),
                pltpu.VMEM((peers, rows, width), returned.dtype),
                pltpu.SemaphoreType.DMA((peers,)),
            ],
        ),
        out_shape=jax.ShapeDtypeStruct((locals_, rows, width), jnp.bfloat16),
        compiler_params=params(),
    )(asked, returned, start)


def exchange(values):
    return lax.all_to_all(values, "nodes", split_axis=0, concat_axis=0, tiled=True)


ASKED, SOURCE, RELAYED, CAME_VIA, WANTED, FITS = range(6)
OPEN = -2


def plan_kernel(
    me_ref, wanted_ref, blocks_ref, plan_ref, out_ref, free_ref, columns_ref, known_ref, sems
):
    peers = wanted_ref.shape[0]
    groups = peers // 8
    me = me_ref[0]
    raw = wanted_ref[...]
    u_ids = lax.broadcasted_iota(jnp.int32, raw.shape, 0)
    named = (raw >= 0).astype(jnp.float32)
    flipped = named.T
    skewed = flipped
    for bit in range(peers.bit_length() - 1):
        turned = pltpu.roll(skewed, peers - (1 << bit), 1)
        skewed = jnp.where(((u_ids >> bit) & 1) == 1, turned, skewed)
    free = (1.0 - skewed.T).astype(jnp.int32)
    free_ref[...] = jnp.broadcast_to(free[:, None, :], free_ref.shape)
    route = jnp.where((named > 0) & (flipped > 0), OPEN, -1)
    spare = 1 - flipped.astype(jnp.int32)
    at_ids = lax.broadcasted_iota(jnp.int32, (8, peers), 0)
    v_ids = lax.broadcasted_iota(jnp.int32, (8, peers), 1)

    def left_open(routes):
        count = (routes[0] == OPEN).astype(jnp.float32)
        for part in routes[1:]:
            count += (part == OPEN).astype(jnp.float32)
        return jnp.sum(count).astype(jnp.int32)

    def one(turn, routes, spares):
        shifts = [(turn + 8 * group) & (peers - 1) for group in range(groups)]
        rooms = [free_ref[shift] for shift in shifts]
        next_routes, next_spares, taken = [], [], []
        for route, spare, shift, room in zip(routes, spares, shifts, rooms):
            fits = (route == OPEN) & ((spare & room) > 0)
            first = jnp.min(jnp.where(fits, at_ids, 8), axis=0, keepdims=True)
            chosen = fits & (at_ids == first)
            taken.append(jnp.where(first < 8, 0, room))
            next_routes.append(jnp.where(chosen, (v_ids + shift) & (peers - 1), route))
            next_spares.append(pltpu.roll(jnp.where(chosen, 0, spare), peers - 1, 1))
        for shift, room in zip(shifts, taken):
            free_ref[shift] = room
        return tuple(next_routes), tuple(next_spares)

    def some(carry):
        turn, _, routes, spares = carry
        for ahead in range(TURNS):
            routes, spares = one(turn + ahead, routes, spares)
        return turn + TURNS, left_open(routes), routes, spares

    routes = tuple(route[8 * group : 8 * group + 8] for group in range(groups))
    spares = tuple(
        pltpu.roll(spare[8 * group : 8 * group + 8], (peers - 8 * group) % peers, 1)
        for group in range(groups)
    )
    _, left, routes, _ = lax.while_loop(
        lambda carry: (carry[0] < peers) & (carry[1] > 0),
        some,
        (jnp.int32(0), left_open(routes), routes, spares),
    )
    route = jnp.concatenate(routes, 0)
    columns = route.astype(jnp.float32).T.astype(jnp.int32)
    columns_ref[...] = columns
    plan_ref[CAME_VIA : CAME_VIA + 1, :] = columns_ref[pl.ds(me, 1), :]
    plan_ref[RELAYED : RELAYED + 1, :] = jnp.max(
        jnp.where(route == me, u_ids, -1), axis=0, keepdims=True
    )
    columns_ref[...] = raw.astype(jnp.float32).T.astype(jnp.int32)
    asked = columns_ref[pl.ds(me, 1), :]
    plan_ref[ASKED : ASKED + 1, :] = asked
    lanes = lax.broadcasted_iota(jnp.int32, raw.shape, 1)
    my_column = lanes == me
    my_vias = jnp.sum(jnp.where(my_column, columns, 0).astype(jnp.float32), 1, keepdims=True)
    my_asked = jnp.sum(jnp.where(my_column, raw, 0).astype(jnp.float32), 1, keepdims=True)
    second = jnp.where(my_vias == lanes.astype(jnp.float32), 2.0 * my_asked + 1.0, 0.0)
    second = jnp.max(second, axis=0, keepdims=True).astype(jnp.int32)
    pieces = 2 * blocks_ref.shape[0]
    plan_ref[SOURCE : SOURCE + 1, :] = jnp.where(asked >= 0, 2 * asked, second) & (pieces - 1)
    plan_ref[WANTED : WANTED + 1, :] = wanted_ref[pl.ds(me, 1), :]
    twice = jnp.sum((raw >= TWICE).astype(jnp.float32)).astype(jnp.int32)
    fits = jnp.where((left == 0) & (twice == 0), 1, 0)
    plan_ref[FITS:, :] = jnp.full((plan_ref.shape[0] - FITS, peers), fits, jnp.int32)
    tell = pltpu.make_async_copy(plan_ref, known_ref, sems.at[0])
    tell.start()
    tell.wait()
    start_first(known_ref, blocks_ref, out_ref, sems.at[1])
    wait_first(out_ref, blocks_ref.shape[1] // 2, sems.at[1])


def make_plan(myself, wanted, blocks):
    peers = wanted.shape[0]
    locals_, rows, width = blocks.shape
    square = pltpu.VMEM((peers, peers), jnp.int32)
    return pl.pallas_call(
        plan_kernel,
        grid_spec=pltpu.PrefetchScalarGridSpec(
            num_scalar_prefetch=1,
            grid=(1,),
            in_specs=[whole(peers, peers), whole(locals_, rows, width)],
            out_specs=[whole(8, peers), pl.BlockSpec(memory_space=pl.ANY)],
            scratch_shapes=[
                pltpu.VMEM((peers, 8, peers), jnp.int32),
                square,
                pltpu.SMEM((8, peers), jnp.int32),
                pltpu.SemaphoreType.DMA((2,)),
            ],
        ),
        out_shape=[
            jax.ShapeDtypeStruct((8, peers), jnp.int32),
            jax.ShapeDtypeStruct((peers, rows // 2, width), blocks.dtype),
        ],
        compiler_params=params(),
    )(jnp.full((1,), myself, jnp.int32), wanted, blocks)


def each_peer(peers, act):
    def step(q, carry):
        act(q)
        return carry

    lax.fori_loop(0, peers, step, 0, unroll=8)


def start_first(plan_ref, blocks_ref, out_ref, sem):
    half = blocks_ref.shape[1] // 2

    def start(q):
        source = plan_ref[SOURCE, q]
        offset = pl.multiple_of((source & 1) * half, half)
        pltpu.make_async_copy(
            blocks_ref.at[source >> 1, pl.ds(offset, half)], out_ref.at[q, pl.ds(0, half)], sem
        ).start()

    each_peer(plan_ref.shape[1], start)


def wait_first(out_ref, half, sem):
    whole_part = out_ref.at[:, pl.ds(0, half)]
    pltpu.make_async_copy(whole_part, whole_part, sem).wait()


def tiles_spec(rows):
    return pl.BlockSpec(
        (GROUP, rows, rows), lambda i, plan, slots: (jnp.minimum(i, slots[3, 0]), 0, 0)
    )


ROW, HOME, COLUMN, LAST = range(4)


def products_kernel(plan_ref, slots_ref, blocks_ref, tiles_ref, out_ref, total_ref):
    step = pl.program_id(0)
    peers = plan_ref.shape[1]
    rows = blocks_ref.shape[1]
    half = rows // 2
    locals_ = blocks_ref.shape[0]

    @pl.when(step == 0)
    def _():
        total_ref[...] = jnp.zeros_like(total_ref)

        def second_half(q):
            @pl.when((plan_ref[ASKED, q] >= 0) & (plan_ref[WANTED, q] < 0))
            def _():
                out_ref[q, pl.ds(0, half)] = blocks_ref[plan_ref[ASKED, q], pl.ds(half, half)]

        each_peer(peers, second_half)

    @pl.when(step <= slots_ref[LAST, 0])
    def _():
        for at in range(GROUP):
            slot = step * GROUP + at
            row, home, column = slots_ref[ROW, slot], slots_ref[HOME, slot], slots_ref[COLUMN, slot]
            tile = tiles_ref[at]
            product = lax.dot_general(
                tile, blocks_ref[row], (((0,), (0,)), ((), ())), preferred_element_type=jnp.float32
            )
            out_ref[home, pl.ds(0, rows)] = product.astype(out_ref.dtype)

            @pl.when(column < locals_)
            def _():
                total_ref[column] += product
                total_ref[row] += jnp.dot(
                    tile, blocks_ref[column], preferred_element_type=jnp.float32
                )


def own_products(plan, slots, blocks, tile_values, extra):
    peers = plan.shape[1]
    slot_total, rows, _ = tile_values.shape
    locals_, _, width = blocks.shape
    return pl.pallas_call(
        products_kernel,
        grid_spec=pltpu.PrefetchScalarGridSpec(
            num_scalar_prefetch=2,
            grid=(slot_total // GROUP,),
            in_specs=[whole(locals_, rows, width), tiles_spec(rows)],
            out_specs=[whole(peers, rows + extra, width), whole(locals_, rows, width)],
        ),
        out_shape=[
            jax.ShapeDtypeStruct((peers, rows + extra, width), blocks.dtype),
            jax.ShapeDtypeStruct((locals_, rows, width), jnp.float32),
        ],
        compiler_params=params(),
        cost_estimate=pl.CostEstimate(
            flops=3 * slot_total * rows * rows * width, bytes_accessed=24 << 20, transcendentals=0
        ),
    )(plan, slots, blocks, tile_values)


def three_parts(value):
    high = value.astype(jnp.bfloat16)
    rest = value - high.astype(jnp.float32)
    middle = rest.astype(jnp.bfloat16)
    low = (rest - middle.astype(jnp.float32)).astype(jnp.bfloat16)
    return [part.astype(jnp.float32) for part in (high, middle, low)]


def relay_kernel(plan_ref, came_ref, _, out_ref, held_ref, sems, *grad_refs):
    peers = plan_ref.shape[1]
    half = came_ref.shape[1] - (EXTRA if grad_refs else 0)

    take = pltpu.make_async_copy(came_ref.at[:, pl.ds(0, half)], held_ref, sems.at[peers])
    take.start()

    def give(q):
        source = jnp.maximum(plan_ref[RELAYED, q], 0)
        return pltpu.make_async_copy(
            held_ref.at[source], out_ref.at[q, pl.ds(half, half)], sems.at[q]
        )

    def turn(q):
        @pl.when(plan_ref[RELAYED, q] >= 0)
        def _():
            give(q).start()

    def wait(q):
        @pl.when(plan_ref[RELAYED, q] >= 0)
        def _():
            give(q).wait()

    if grad_refs:
        (staged_ref,) = grad_refs
        bring = pltpu.make_async_copy(
            came_ref.at[:, pl.ds(half, EXTRA)], staged_ref, sems.at[peers + 1]
        )
        bring.start()
    take.wait()
    each_peer(peers, turn)
    if grad_refs:
        bring.wait()
        sums = jnp.sum(staged_ref[...].astype(jnp.float32), axis=0)
        own = (sums[4:6] + sums[2:4]) + sums[0:2]
        parts = three_parts(own)
        packed = jnp.concatenate(parts + [jnp.zeros((EXTRA - 6, own.shape[1]), jnp.float32)], 0)
        staged_ref[...] = jnp.broadcast_to(packed[None], staged_ref.shape).astype(jnp.bfloat16)
        put = pltpu.make_async_copy(
            staged_ref, out_ref.at[:, pl.ds(2 * half, EXTRA)], sems.at[peers + 2]
        )
        put.start()
        put.wait()
    each_peer(peers, wait)


def relay(plan, came, outgoing, with_grad):
    peers, _, width = came.shape
    scratch = [
        pltpu.VMEM((peers, came.shape[1] - (EXTRA if with_grad else 0), width), came.dtype),
        pltpu.SemaphoreType.DMA((peers + 3,)),
    ]
    if with_grad:
        scratch.append(pltpu.VMEM((peers, EXTRA, width), jnp.bfloat16))
    anywhere = pl.BlockSpec(memory_space=pl.ANY)
    return pl.pallas_call(
        relay_kernel,
        grid_spec=pltpu.PrefetchScalarGridSpec(
            num_scalar_prefetch=1,
            grid=(1,),
            in_specs=[anywhere, anywhere],
            out_specs=anywhere,
            scratch_shapes=scratch,
        ),
        out_shape=jax.ShapeDtypeStruct(outgoing.shape, outgoing.dtype),
        input_output_aliases={2: 0},
        compiler_params=params(),
    )(plan, came, outgoing)


def early_kernel(plan_ref, slots_ref, first_ref, tiles_ref, start_ref, total_ref, sums_ref):
    step = pl.program_id(0)
    half = tiles_ref.shape[2]
    locals_ = start_ref.shape[0]

    @pl.when(step == 0)
    def _():
        sums_ref[pl.ds(0, locals_)] = start_ref[...]

    @pl.when(step <= slots_ref[LAST, 0])
    def _():
        for at in range(GROUP):
            slot = step * GROUP + at
            remote = slots_ref[COLUMN, slot] == locals_
            row = jnp.where(remote, slots_ref[ROW, slot], locals_)
            sums_ref[row] += jnp.dot(
                tiles_ref[at],
                first_ref[slots_ref[HOME, slot], pl.ds(0, half)],
                preferred_element_type=jnp.float32,
            )

    @pl.when(step == pl.num_programs(0) - 1)
    def _():
        total_ref[...] = sums_ref[pl.ds(0, locals_)]


def early_products(plan, slots, first, tile_values, start):
    slot_total, rows, _ = tile_values.shape
    locals_, _, width = start.shape
    return pl.pallas_call(
        early_kernel,
        grid_spec=pltpu.PrefetchScalarGridSpec(
            num_scalar_prefetch=2,
            grid=(slot_total // GROUP,),
            in_specs=[
                whole(*first.shape),
                pl.BlockSpec(
                    (GROUP, rows, rows // 2),
                    lambda i, plan, slots: (jnp.minimum(i, slots[LAST, 0]), 0, 0),
                ),
                whole(*start.shape),
            ],
            out_specs=whole(*start.shape),
            scratch_shapes=[pltpu.VMEM((locals_ + 1, rows, width), jnp.float32)],
        ),
        out_shape=jax.ShapeDtypeStruct(start.shape, start.dtype),
        compiler_params=params(),
        cost_estimate=pl.CostEstimate(
            flops=slot_total * rows * rows * width, bytes_accessed=12 << 20, transcendentals=0
        ),
    )(plan, slots, first, tile_values, start)


def late_scratch(second, tile_values, start):
    peers, _, width = second.shape
    slot_total, rows, _ = tile_values.shape
    return [
        pltpu.VMEM((start.shape[0] + 1, rows, width), jnp.float32),
        pltpu.VMEM(second.shape, second.dtype),
        pltpu.VMEM((slot_total, rows, rows // 2), tile_values.dtype),
        pltpu.SemaphoreType.DMA((PARTS + slot_total // GROUP + 1,)),
    ]


def late_sums(plan_ref, slots_ref, second_ref, tiles_ref, start_ref, total_ref, landed_ref, held_ref, sems):
    peers = plan_ref.shape[1]
    slot_total, rows, half = held_ref.shape
    locals_ = start_ref.shape[0]
    share = peers // PARTS

    def landing(part):
        piece = pl.ds(part * share, share)
        return pltpu.make_async_copy(second_ref.at[piece], landed_ref.at[piece], sems.at[part])

    def holding(group):
        piece = pl.ds(group * GROUP, GROUP)
        return pltpu.make_async_copy(
            tiles_ref.at[piece, :, pl.ds(half, half)], held_ref.at[piece], sems.at[PARTS + group]
        )

    groups = slot_total // GROUP
    begin = pltpu.make_async_copy(
        start_ref, total_ref.at[pl.ds(0, locals_)], sems.at[PARTS + groups]
    )
    begin.start()
    for part in range(PARTS):
        landing(part).start()
    for group in range(groups):

        @pl.when(group <= slots_ref[LAST, 0])
        def _():
            holding(group).start()

    begin.wait()

    def add(q, carry):
        block = plan_ref[ASKED, q]

        @pl.when(block >= 0)
        def _():
            total_ref[block] += landed_ref[q, pl.ds(0, rows)].astype(jnp.float32)

        return carry

    for part in range(PARTS):
        landing(part).wait()
        lax.fori_loop(part * share, (part + 1) * share, add, 0, unroll=4)

    def multiply(group, carry):
        @pl.when(group <= slots_ref[LAST, 0])
        def _():
            holding(group).wait()
            for at in range(GROUP):
                slot = group * GROUP + at
                home = slots_ref[HOME, slot]
                remote = slots_ref[COLUMN, slot] == locals_
                row = jnp.where(remote, slots_ref[ROW, slot], locals_)
                via = plan_ref[CAME_VIA, home]
                source = jnp.where(via >= 0, via, home)
                offset = pl.multiple_of(jnp.where(via >= 0, half, 0), half)
                total_ref[row] += jnp.dot(
                    held_ref[slot],
                    landed_ref[source, pl.ds(offset, half)],
                    preferred_element_type=jnp.float32,
                )

        return carry

    lax.fori_loop(0, groups, multiply, 0)


def layer_kernel(
    plan_ref,
    slots_ref,
    second_ref,
    tiles_ref,
    start_ref,
    weight_ref,
    cotangent_ref,
    hidden_ref,
    upstream_ref,
    out_ref,
    total_ref,
    landed_ref,
    held_ref,
    late_sems,
    grad_ref,
    rows_ref,
    staged_ref,
    gradient_ref,
    result_ref,
    back_ref,
    sems,
):
    locals_ = total_ref.shape[0] - 1
    bring = pltpu.make_async_copy(cotangent_ref, gradient_ref, sems.at[2 * locals_])
    bring.start()
    late_sums(
        plan_ref,
        slots_ref,
        second_ref,
        tiles_ref,
        start_ref,
        total_ref,
        landed_ref,
        held_ref,
        late_sems,
    )
    peers = plan_ref.shape[1]
    half = held_ref.shape[2]
    width = upstream_ref.shape[2]
    weight = weight_ref[...]
    grad_ref[...] = jnp.zeros_like(grad_ref)
    bring.wait()

    def give(k):
        return (
            pltpu.make_async_copy(result_ref.at[k], hidden_ref.at[k], sems.at[k]),
            pltpu.make_async_copy(back_ref.at[k], upstream_ref.at[k], sems.at[locals_ + k]),
        )

    def block_step(k, carry):
        aggregated = total_ref[k].astype(jnp.bfloat16)
        preact = jnp.dot(aggregated, weight, preferred_element_type=jnp.float32)
        sigma = 1.0 / (1.0 + jnp.exp(-preact))
        result_ref[k] = (preact * sigma).astype(jnp.bfloat16)
        delta = (
            gradient_ref[k].astype(jnp.float32) * sigma * (1.0 + preact * (1.0 - sigma))
        ).astype(jnp.bfloat16)
        grad_ref[...] += lax.dot_general(
            aggregated, delta, (((0,), (0,)), ((), ())), preferred_element_type=jnp.float32
        )
        back_ref[k] = lax.dot_general(
            delta, weight, (((1,), (1,)), ((), ())), preferred_element_type=jnp.float32
        ).astype(jnp.bfloat16)
        for copy in give(k):
            copy.start()
        return carry

    lax.fori_loop(0, locals_, block_step, 0, unroll=2)
    start_first(plan_ref, back_ref, out_ref, sems.at[2 * locals_ + 1])
    for side in range(2):
        parts = three_parts(grad_ref[:, side * width : (side + 1) * width])
        for at, part in enumerate(parts):
            rows_ref[:, 2 * at + side, :] = part
    for at in range(6, EXTRA):
        rows_ref[:, at, :] = jnp.zeros((peers, width), jnp.float32)
    staged_ref[...] = rows_ref[...].astype(jnp.bfloat16)
    put = pltpu.make_async_copy(
        staged_ref, out_ref.at[:, pl.ds(half, EXTRA)], sems.at[2 * locals_ + 2]
    )
    put.start()
    for k in range(locals_):
        for copy in give(k):
            copy.wait()
    wait_first(out_ref, half, sems.at[2 * locals_ + 1])
    put.wait()


def layer(plan, slots, second, tile_values, start, weight, cotangent):
    peers, _, width = second.shape
    _, rows, _ = tile_values.shape
    locals_ = start.shape[0]
    hid = weight.shape[1]
    assert width == peers and hid == 2 * width
    anywhere = pl.BlockSpec(memory_space=pl.ANY)
    return pl.pallas_call(
        layer_kernel,
        grid_spec=pltpu.PrefetchScalarGridSpec(
            num_scalar_prefetch=2,
            grid=(1,),
            in_specs=[anywhere, anywhere, anywhere, whole(width, hid), anywhere],
            out_specs=[anywhere, anywhere, anywhere],
            scratch_shapes=late_scratch(second, tile_values, start)
            + [
                pltpu.VMEM((width, hid), jnp.float32),
                pltpu.VMEM((peers, EXTRA, width), jnp.float32),
                pltpu.VMEM((peers, EXTRA, width), jnp.bfloat16),
                pltpu.VMEM((locals_, rows, hid), jnp.bfloat16),
                pltpu.VMEM((locals_, rows, hid), jnp.bfloat16),
                pltpu.VMEM((locals_, rows, width), jnp.bfloat16),
                pltpu.SemaphoreType.DMA((2 * locals_ + 3,)),
            ],
        ),
        out_shape=[
            jax.ShapeDtypeStruct((locals_, rows, hid), jnp.bfloat16),
            jax.ShapeDtypeStruct((locals_, rows, width), jnp.bfloat16),
            jax.ShapeDtypeStruct((peers, rows // 2 + EXTRA, width), jnp.bfloat16),
        ],
        compiler_params=params(),
    )(plan, slots, second, tile_values, start, weight, cotangent)


def last_kernel(
    scale,
    plan_ref,
    slots_ref,
    second_ref,
    tiles_ref,
    start_ref,
    out_ref,
    weight_grad_ref,
    total_ref,
    landed_ref,
    held_ref,
    late_sems,
    rows_ref,
):
    late_sums(
        plan_ref,
        slots_ref,
        second_ref,
        tiles_ref,
        start_ref,
        total_ref,
        landed_ref,
        held_ref,
        late_sems,
    )
    rows = held_ref.shape[1]
    width = out_ref.shape[2]
    out_ref[...] = total_ref[pl.ds(0, out_ref.shape[0])].astype(out_ref.dtype)
    rows_ref[...] = landed_ref[:, pl.ds(rows, EXTRA)].astype(jnp.float32)
    for side in range(2):
        weight_grad_ref[:, side * width : (side + 1) * width] = (
            rows_ref[:, 4 + side, :] + rows_ref[:, 2 + side, :] + rows_ref[:, side, :]
        ) * scale


def last(plan, slots, second, tile_values, start, scale):
    peers, _, width = second.shape
    _, rows, _ = tile_values.shape
    locals_ = start.shape[0]
    anywhere = pl.BlockSpec(memory_space=pl.ANY)
    return pl.pallas_call(
        functools.partial(last_kernel, scale),
        grid_spec=pltpu.PrefetchScalarGridSpec(
            num_scalar_prefetch=2,
            grid=(1,),
            in_specs=[anywhere, anywhere, anywhere],
            out_specs=[whole(locals_, rows, width), whole(peers, 2 * width)],
            scratch_shapes=late_scratch(second, tile_values, start)
            + [pltpu.VMEM((peers, EXTRA, width), jnp.float32)],
        ),
        out_shape=[
            jax.ShapeDtypeStruct((locals_, rows, width), jnp.bfloat16),
            jax.ShapeDtypeStruct((peers, 2 * width), jnp.float32),
        ],
        compiler_params=params(),
    )(plan, slots, second, tile_values, start)


def on_device(features, weight, cotangent, block_pairs, tile_counts, tile_values):
    peers = lax.axis_size("nodes")
    myself = lax.axis_index("nodes")
    rows = tile_values.shape[1]
    width = features.shape[1]
    hid = weight.shape[1]
    locals_ = features.shape[0] // rows
    count = tile_counts[0]
    slot_ids = jnp.arange(block_pairs.shape[0], dtype=jnp.int32)
    peer_ids = jnp.arange(peers, dtype=jnp.int32)
    row_local = jnp.clip(block_pairs[:, 0] - myself * locals_, 0, locals_ - 1)
    col_blocks = block_pairs[:, 1]
    home = col_blocks // locals_
    column = col_blocks % locals_
    live = slot_ids < count
    remote = live & (home != myself)
    hit = (home[None, :] == peer_ids[:, None]) & remote[None, :]
    wanted = jnp.max(jnp.where(hit, column[None, :], -1), axis=1)
    named_twice = jnp.sum(hit.astype(jnp.int32), axis=1) > 1
    wanted = wanted + jnp.where(named_twice, TWICE, 0)
    everyones = exchange(jnp.broadcast_to(wanted[None, :], (peers, peers)))
    blocks = features.reshape(locals_, rows, width)
    plan, sending = make_plan(myself, everyones, blocks)
    cotangent_blocks = cotangent.reshape(locals_, rows, hid)
    scale = 1.0 / math.sqrt(peers * locals_ * rows)

    def sparse():
        slots = jnp.stack(
            [
                row_local,
                jnp.where(remote, home, myself),
                jnp.where(live & ~remote, column, jnp.where(remote, locals_, locals_ + 1)),
                jnp.broadcast_to((count - 1) // GROUP, row_local.shape),
            ]
        )
        first = exchange(sending)
        outgoing, total = own_products(plan, slots, blocks, tile_values, 0)
        first, outgoing = lax.optimization_barrier((first, outgoing))
        second = exchange(relay(plan, first, outgoing, False))
        total = early_products(plan, slots, first, tile_values, total)
        hidden, upstream, halves = layer(
            plan, slots, second, tile_values, total, weight, cotangent_blocks
        )
        first = exchange(halves)
        outgoing, total = own_products(plan, slots, upstream, tile_values, EXTRA)
        first, outgoing = lax.optimization_barrier((first, outgoing))
        second = exchange(relay(plan, first, outgoing, True))
        total = early_products(plan, slots, first, tile_values, total)
        feature_grad, weight_grad = last(plan, slots, second, tile_values, total, scale)
        return hidden, weight_grad, feature_grad

    def full():
        asked = plan[ASKED]
        asked = jnp.where(asked >= 0, asked % TWICE, -1)
        dest = jnp.where(live, jnp.where(remote, home, peers + column), -1)
        earlier = (home[None, :] == home[:, None]) & (slot_ids[None, :] < slot_ids[:, None])
        again = jnp.any(earlier, axis=1).astype(jnp.int32)
        arrived = exchange(pick(asked, blocks))
        outgoing, total = transposed_products(row_local, dest, again, blocks, tile_values, peers)
        returned = exchange(outgoing)
        total = direct_products(row_local, dest, arrived, tile_values, total)
        hidden, local_grad, upstream, requested = dense(
            asked, returned, total, weight, cotangent_blocks
        )
        row_sum = jnp.sum(exchange(local_grad), axis=0) * scale
        weight_grad = exchange(jnp.broadcast_to(row_sum, local_grad.shape))
        arrived = exchange(requested)
        outgoing, total = transposed_products(row_local, dest, again, upstream, tile_values, peers)
        returned = exchange(outgoing)
        total = direct_products(row_local, dest, arrived, tile_values, total)
        return hidden, weight_grad, finish(asked, returned, total)

    hidden, weight_grad, feature_grad = lax.cond(plan[FITS, 0] > 0, sparse, full)
    return (
        hidden.reshape(locals_ * rows, hid),
        weight_grad,
        feature_grad.reshape(locals_ * rows, width),
    )


def solution(mesh):
    return jax.shard_map(
        on_device,
        mesh=mesh,
        in_specs=(
            P("nodes", None),
            P(),
            P("nodes", None),
            P("nodes", None),
            P("nodes"),
            P("nodes", None, None),
        ),
        out_specs=(P("nodes", None), P(), P("nodes", None)),
        check_vma=False,
    )
```

```python
import functools
import math

import jax
import jax.numpy as jnp
from jax import lax
from jax.experimental import pallas as pl
from jax.experimental.pallas import tpu as pltpu
from jax.sharding import PartitionSpec as P

VMEM_LIMIT = 60 * 1024 * 1024
GROUP = 16
PARTS = 4
EXTRA = 16
TWICE = 64
TURNS = 8


def whole(*shape):
    return pl.BlockSpec(shape, lambda *_: (0,) * len(shape), pipeline_mode=pl.Buffered(1))


def params(limit=VMEM_LIMIT):
    return pltpu.CompilerParams(vmem_limit_bytes=limit)


def send_blocks(asked_ref, blocks_ref, out_ref, sems):
    def copy(q):
        block = jnp.maximum(asked_ref[q], 0)
        return pltpu.make_async_copy(blocks_ref.at[block], out_ref.at[q], sems.at[q])

    def start(q, carry):
        @pl.when(asked_ref[q] >= 0)
        def _():
            copy(q).start()

        return carry

    def wait(q, carry):
        @pl.when(asked_ref[q] >= 0)
        def _():
            copy(q).wait()

        return carry

    peers = asked_ref.shape[0]
    lax.fori_loop(0, peers, start, 0)
    lax.fori_loop(0, peers, wait, 0)


def pick(asked, blocks):
    peers = asked.shape[0]
    locals_, rows, width = blocks.shape
    return pl.pallas_call(
        send_blocks,
        grid_spec=pltpu.PrefetchScalarGridSpec(
            num_scalar_prefetch=1,
            grid=(1,),
            in_specs=[whole(locals_, rows, width)],
            out_specs=pl.BlockSpec(memory_space=pl.ANY),
            scratch_shapes=[pltpu.SemaphoreType.DMA((peers,))],
        ),
        out_shape=jax.ShapeDtypeStruct((peers, rows, width), blocks.dtype),
        compiler_params=params(),
    )(asked, blocks)


def transposed_kernel(
    peers, row_ref, dest_ref, again_ref, blocks_ref, tiles_ref, out_ref, total_ref
):
    step = pl.program_id(0)

    @pl.when(step == 0)
    def _():
        total_ref[...] = jnp.zeros_like(total_ref)

    def visit(at, carry):
        slot = step * GROUP + at
        dest = dest_ref[slot]

        @pl.when(dest >= 0)
        def _():
            row = row_ref[slot]
            product = lax.dot_general(
                tiles_ref[at],
                blocks_ref[row],
                (((0,), (0,)), ((), ())),
                preferred_element_type=jnp.float32,
            )
            remote = dest < peers

            @pl.when(remote & (again_ref[slot] == 0))
            def _():
                out_ref[dest] = product.astype(out_ref.dtype)

            @pl.when(remote & (again_ref[slot] == 1))
            def _():
                out_ref[dest] = (out_ref[dest].astype(jnp.float32) + product).astype(out_ref.dtype)

            @pl.when(jnp.logical_not(remote))
            def _():
                column = dest - peers
                total_ref[column] += product
                total_ref[row] += jnp.dot(
                    tiles_ref[at], blocks_ref[column], preferred_element_type=jnp.float32
                )

        return carry

    lax.fori_loop(0, GROUP, visit, 0)


def transposed_products(row_local, dest, again, blocks, tile_values, peers):
    slots, rows, _ = tile_values.shape
    locals_, _, width = blocks.shape
    return pl.pallas_call(
        functools.partial(transposed_kernel, peers),
        grid_spec=pltpu.PrefetchScalarGridSpec(
            num_scalar_prefetch=3,
            grid=(slots // GROUP,),
            in_specs=[
                whole(locals_, rows, width),
                pl.BlockSpec((GROUP, rows, rows), lambda i, *_: (i, 0, 0)),
            ],
            out_specs=[whole(peers, rows, width), whole(locals_, rows, width)],
        ),
        out_shape=[
            jax.ShapeDtypeStruct((peers, rows, width), blocks.dtype),
            jax.ShapeDtypeStruct((locals_, rows, width), jnp.float32),
        ],
        compiler_params=params(),
        cost_estimate=pl.CostEstimate(
            flops=3 * slots * rows * rows * width, bytes_accessed=24 << 20, transcendentals=0
        ),
    )(row_local, dest, again, blocks, tile_values)


def direct_kernel(peers, row_ref, dest_ref, arrived_ref, tiles_ref, start_ref, total_ref):
    step = pl.program_id(0)

    @pl.when(step == 0)
    def _():
        total_ref[...] = start_ref[...]

    def visit(at, carry):
        slot = step * GROUP + at
        source = dest_ref[slot]

        @pl.when((source >= 0) & (source < peers))
        def _():
            total_ref[row_ref[slot]] += jnp.dot(
                tiles_ref[at], arrived_ref[source], preferred_element_type=jnp.float32
            )

        return carry

    lax.fori_loop(0, GROUP, visit, 0)


def direct_products(row_local, dest, arrived, tile_values, start):
    slots, rows, _ = tile_values.shape
    peers, _, width = arrived.shape
    locals_ = start.shape[0]
    return pl.pallas_call(
        functools.partial(direct_kernel, peers),
        grid_spec=pltpu.PrefetchScalarGridSpec(
            num_scalar_prefetch=2,
            grid=(slots // GROUP,),
            in_specs=[
                whole(peers, rows, width),
                pl.BlockSpec((GROUP, rows, rows), lambda i, *_: (i, 0, 0)),
                whole(locals_, rows, width),
            ],
            out_specs=whole(locals_, rows, width),
        ),
        out_shape=jax.ShapeDtypeStruct((locals_, rows, width), jnp.float32),
        compiler_params=params(),
        cost_estimate=pl.CostEstimate(
            flops=2 * slots * rows * rows * width, bytes_accessed=24 << 20, transcendentals=0
        ),
    )(row_local, dest, arrived, tile_values, start)


def add_returned(asked_ref, returned_ref, start_ref, total_ref, landed_ref, sems):
    def copy(q):
        return pltpu.make_async_copy(returned_ref.at[q], landed_ref.at[q], sems.at[q])

    def start(q, carry):
        @pl.when(asked_ref[q] >= 0)
        def _():
            copy(q).start()

        return carry

    def add(q, carry):
        block = asked_ref[q]

        @pl.when(block >= 0)
        def _():
            copy(q).wait()
            total_ref[block] += landed_ref[q].astype(jnp.float32)

        return carry

    peers = asked_ref.shape[0]
    lax.fori_loop(0, peers, start, 0)
    total_ref[...] = start_ref[...]
    lax.fori_loop(0, peers, add, 0)


def dense_kernel(
    asked_ref,
    returned_ref,
    start_ref,
    weight_ref,
    cotangent_ref,
    hidden_ref,
    grad_ref,
    upstream_ref,
    out_ref,
    total_ref,
    landed_ref,
    sems,
):
    add_returned(asked_ref, returned_ref, start_ref, total_ref, landed_ref, sems)
    grad_ref[...] = jnp.zeros_like(grad_ref)
    weight = weight_ref[...]

    def block_step(k, carry):
        aggregated = total_ref[k].astype(jnp.bfloat16)
        preact = jnp.dot(aggregated, weight, preferred_element_type=jnp.float32)
        sigma = 1.0 / (1.0 + jnp.exp(-preact))
        hidden_ref[k] = (preact * sigma).astype(jnp.bfloat16)
        delta = (
            cotangent_ref[k].astype(jnp.float32) * sigma * (1.0 + preact * (1.0 - sigma))
        ).astype(jnp.bfloat16)
        grad_ref[...] += lax.dot_general(
            aggregated, delta, (((0,), (0,)), ((), ())), preferred_element_type=jnp.float32
        )
        upstream_ref[k] = lax.dot_general(
            delta, weight, (((1,), (1,)), ((), ())), preferred_element_type=jnp.float32
        ).astype(jnp.bfloat16)
        return carry

    lax.fori_loop(0, total_ref.shape[0], block_step, 0)
    send_blocks(asked_ref, upstream_ref, out_ref, sems)


def dense(asked, returned, start, weight, cotangent):
    peers, rows, width = returned.shape
    locals_ = start.shape[0]
    hid = weight.shape[1]
    return pl.pallas_call(
        dense_kernel,
        grid_spec=pltpu.PrefetchScalarGridSpec(
            num_scalar_prefetch=1,
            grid=(1,),
            in_specs=[
                pl.BlockSpec(memory_space=pl.ANY),
                whole(locals_, rows, width),
                whole(width, hid),
                whole(locals_, rows, hid),
            ],
            out_specs=[
                whole(locals_, rows, hid),
                whole(width, hid),
                whole(locals_, rows, width),
                pl.BlockSpec(memory_space=pl.ANY),
            ],
            scratch_shapes=[
                pltpu.VMEM((locals_, rows, width), jnp.float32),
                pltpu.VMEM((peers, rows, width), returned.dtype),
                pltpu.SemaphoreType.DMA((peers,)),
            ],
        ),
        out_shape=[
            jax.ShapeDtypeStruct((locals_, rows, hid), jnp.bfloat16),
            jax.ShapeDtypeStruct((width, hid), jnp.float32),
            jax.ShapeDtypeStruct((locals_, rows, width), jnp.bfloat16),
            jax.ShapeDtypeStruct((peers, rows, width), jnp.bfloat16),
        ],
        compiler_params=params(),
    )(asked, returned, start, weight, cotangent)


def finish_kernel(asked_ref, returned_ref, start_ref, out_ref, total_ref, landed_ref, sems):
    add_returned(asked_ref, returned_ref, start_ref, total_ref, landed_ref, sems)
    out_ref[...] = total_ref[...].astype(out_ref.dtype)


def finish(asked, returned, start):
    peers, rows, width = returned.shape
    locals_ = start.shape[0]
    return pl.pallas_call(
        finish_kernel,
        grid_spec=pltpu.PrefetchScalarGridSpec(
            num_scalar_prefetch=1,
            grid=(1,),
            in_specs=[pl.BlockSpec(memory_space=pl.ANY), whole(locals_, rows, width)],
            out_specs=whole(locals_, rows, width),
            scratch_shapes=[
                pltpu.VMEM((locals_, rows, width), jnp.float32),
                pltpu.VMEM((peers, rows, width), returned.dtype),
                pltpu.SemaphoreType.DMA((peers,)),
            ],
        ),
        out_shape=jax.ShapeDtypeStruct((locals_, rows, width), jnp.bfloat16),
        compiler_params=params(),
    )(asked, returned, start)


def exchange(values):
    return lax.all_to_all(values, "nodes", split_axis=0, concat_axis=0, tiled=True)


ASKED, SOURCE, RELAYED, CAME_VIA, WANTED, FITS = range(6)
OPEN = -2


def plan_kernel(
    me_ref, wanted_ref, blocks_ref, plan_ref, out_ref, free_ref, columns_ref, known_ref, sems
):
    peers = wanted_ref.shape[0]
    groups = peers // 8
    me = me_ref[0]
    raw = wanted_ref[...]
    u_ids = lax.broadcasted_iota(jnp.int32, raw.shape, 0)
    named = (raw >= 0).astype(jnp.float32)
    flipped = named.T
    skewed = flipped
    for bit in range(peers.bit_length() - 1):
        turned = pltpu.roll(skewed, peers - (1 << bit), 1)
        skewed = jnp.where(((u_ids >> bit) & 1) == 1, turned, skewed)
    free = (1.0 - skewed.T).astype(jnp.int32)
    free_ref[...] = jnp.broadcast_to(free[:, None, :], free_ref.shape)
    route = jnp.where((named > 0) & (flipped > 0), OPEN, -1)
    spare = 1 - flipped.astype(jnp.int32)
    needs = jnp.sum((route == OPEN).astype(jnp.float32), axis=1, keepdims=True).astype(jnp.int32)
    ranks = (peers - needs) * 8 + (u_ids & 7)
    ranks = [ranks[8 * group : 8 * group + 8] for group in range(groups)]
    lowest = 16 * peers
    v_ids = lax.broadcasted_iota(jnp.int32, (8, peers), 1)

    def left_open(routes):
        count = (routes[0] == OPEN).astype(jnp.float32)
        for part in routes[1:]:
            count += (part == OPEN).astype(jnp.float32)
        return jnp.sum(count).astype(jnp.int32)

    def one(turn, routes, spares):
        shifts = [(turn + 8 * group) & (peers - 1) for group in range(groups)]
        rooms = [free_ref[shift] for shift in shifts]
        next_routes, next_spares, taken = [], [], []
        for route, spare, rank, shift, room in zip(routes, spares, ranks, shifts, rooms):
            fits = (route == OPEN) & ((spare & room) > 0)
            first = jnp.min(jnp.where(fits, rank, lowest), axis=0, keepdims=True)
            chosen = fits & (rank == first)
            taken.append(jnp.where(first < lowest, 0, room))
            next_routes.append(jnp.where(chosen, (v_ids + shift) & (peers - 1), route))
            next_spares.append(pltpu.roll(jnp.where(chosen, 0, spare), peers - 1, 1))
        for shift, room in zip(shifts, taken):
            free_ref[shift] = room
        return tuple(next_routes), tuple(next_spares)

    def some(carry):
        turn, _, routes, spares = carry
        for ahead in range(TURNS):
            routes, spares = one(turn + ahead, routes, spares)
        return turn + TURNS, left_open(routes), routes, spares

    routes = tuple(route[8 * group : 8 * group + 8] for group in range(groups))
    spares = tuple(
        pltpu.roll(spare[8 * group : 8 * group + 8], (peers - 8 * group) % peers, 1)
        for group in range(groups)
    )
    _, left, routes, _ = lax.while_loop(
        lambda carry: (carry[0] < peers) & (carry[1] > 0),
        some,
        (jnp.int32(0), left_open(routes), routes, spares),
    )
    route = jnp.concatenate(routes, 0)
    columns = route.astype(jnp.float32).T.astype(jnp.int32)
    columns_ref[...] = columns
    plan_ref[CAME_VIA : CAME_VIA + 1, :] = columns_ref[pl.ds(me, 1), :]
    plan_ref[RELAYED : RELAYED + 1, :] = jnp.max(
        jnp.where(route == me, u_ids, -1), axis=0, keepdims=True
    )
    columns_ref[...] = raw.astype(jnp.float32).T.astype(jnp.int32)
    asked = columns_ref[pl.ds(me, 1), :]
    plan_ref[ASKED : ASKED + 1, :] = asked
    lanes = lax.broadcasted_iota(jnp.int32, raw.shape, 1)
    my_column = lanes == me
    my_vias = jnp.sum(jnp.where(my_column, columns, 0).astype(jnp.float32), 1, keepdims=True)
    my_asked = jnp.sum(jnp.where(my_column, raw, 0).astype(jnp.float32), 1, keepdims=True)
    second = jnp.where(my_vias == lanes.astype(jnp.float32), 2.0 * my_asked + 1.0, 0.0)
    second = jnp.max(second, axis=0, keepdims=True).astype(jnp.int32)
    pieces = 2 * blocks_ref.shape[0]
    plan_ref[SOURCE : SOURCE + 1, :] = jnp.where(asked >= 0, 2 * asked, second) & (pieces - 1)
    plan_ref[WANTED : WANTED + 1, :] = wanted_ref[pl.ds(me, 1), :]
    twice = jnp.sum((raw >= TWICE).astype(jnp.float32)).astype(jnp.int32)
    fits = jnp.where((left == 0) & (twice == 0), 1, 0)
    plan_ref[FITS:, :] = jnp.full((plan_ref.shape[0] - FITS, peers), fits, jnp.int32)
    tell = pltpu.make_async_copy(plan_ref, known_ref, sems.at[0])
    tell.start()
    tell.wait()
    start_first(known_ref, blocks_ref, out_ref, sems.at[1])
    wait_first(out_ref, blocks_ref.shape[1] // 2, sems.at[1])


def make_plan(myself, wanted, blocks):
    peers = wanted.shape[0]
    locals_, rows, width = blocks.shape
    square = pltpu.VMEM((peers, peers), jnp.int32)
    return pl.pallas_call(
        plan_kernel,
        grid_spec=pltpu.PrefetchScalarGridSpec(
            num_scalar_prefetch=1,
            grid=(1,),
            in_specs=[whole(peers, peers), whole(locals_, rows, width)],
            out_specs=[whole(8, peers), pl.BlockSpec(memory_space=pl.ANY)],
            scratch_shapes=[
                pltpu.VMEM((peers, 8, peers), jnp.int32),
                square,
                pltpu.SMEM((8, peers), jnp.int32),
                pltpu.SemaphoreType.DMA((2,)),
            ],
        ),
        out_shape=[
            jax.ShapeDtypeStruct((8, peers), jnp.int32),
            jax.ShapeDtypeStruct((peers, rows // 2, width), blocks.dtype),
        ],
        compiler_params=params(),
    )(jnp.full((1,), myself, jnp.int32), wanted, blocks)


def each_peer(peers, act):
    def step(q, carry):
        act(q)
        return carry

    lax.fori_loop(0, peers, step, 0, unroll=8)


def start_first(plan_ref, blocks_ref, out_ref, sem):
    half = blocks_ref.shape[1] // 2

    def start(q):
        source = plan_ref[SOURCE, q]
        offset = pl.multiple_of((source & 1) * half, half)
        pltpu.make_async_copy(
            blocks_ref.at[source >> 1, pl.ds(offset, half)], out_ref.at[q, pl.ds(0, half)], sem
        ).start()

    each_peer(plan_ref.shape[1], start)


def wait_first(out_ref, half, sem):
    whole_part = out_ref.at[:, pl.ds(0, half)]
    pltpu.make_async_copy(whole_part, whole_part, sem).wait()


def tiles_spec(rows):
    return pl.BlockSpec(
        (GROUP, rows, rows), lambda i, plan, slots: (jnp.minimum(i, slots[3, 0]), 0, 0)
    )


ROW, HOME, COLUMN, LAST = range(4)


def products_kernel(plan_ref, slots_ref, blocks_ref, tiles_ref, out_ref, total_ref):
    step = pl.program_id(0)
    peers = plan_ref.shape[1]
    rows = blocks_ref.shape[1]
    half = rows // 2
    locals_ = blocks_ref.shape[0]

    @pl.when(step == 0)
    def _():
        total_ref[...] = jnp.zeros_like(total_ref)

        def second_half(q):
            @pl.when((plan_ref[ASKED, q] >= 0) & (plan_ref[WANTED, q] < 0))
            def _():
                out_ref[q, pl.ds(0, half)] = blocks_ref[plan_ref[ASKED, q], pl.ds(half, half)]

        each_peer(peers, second_half)

    @pl.when(step <= slots_ref[LAST, 0])
    def _():
        for at in range(GROUP):
            slot = step * GROUP + at
            row, home, column = slots_ref[ROW, slot], slots_ref[HOME, slot], slots_ref[COLUMN, slot]
            tile = tiles_ref[at]
            product = lax.dot_general(
                tile, blocks_ref[row], (((0,), (0,)), ((), ())), preferred_element_type=jnp.float32
            )
            out_ref[home, pl.ds(0, rows)] = product.astype(out_ref.dtype)

            @pl.when(column < locals_)
            def _():
                total_ref[column] += product
                total_ref[row] += jnp.dot(
                    tile, blocks_ref[column], preferred_element_type=jnp.float32
                )


def own_products(plan, slots, blocks, tile_values, extra):
    peers = plan.shape[1]
    slot_total, rows, _ = tile_values.shape
    locals_, _, width = blocks.shape
    return pl.pallas_call(
        products_kernel,
        grid_spec=pltpu.PrefetchScalarGridSpec(
            num_scalar_prefetch=2,
            grid=(slot_total // GROUP,),
            in_specs=[whole(locals_, rows, width), tiles_spec(rows)],
            out_specs=[whole(peers, rows + extra, width), whole(locals_, rows, width)],
        ),
        out_shape=[
            jax.ShapeDtypeStruct((peers, rows + extra, width), blocks.dtype),
            jax.ShapeDtypeStruct((locals_, rows, width), jnp.float32),
        ],
        compiler_params=params(),
        cost_estimate=pl.CostEstimate(
            flops=3 * slot_total * rows * rows * width, bytes_accessed=24 << 20, transcendentals=0
        ),
    )(plan, slots, blocks, tile_values)


def three_parts(value):
    high = value.astype(jnp.bfloat16)
    rest = value - high.astype(jnp.float32)
    middle = rest.astype(jnp.bfloat16)
    low = (rest - middle.astype(jnp.float32)).astype(jnp.bfloat16)
    return [part.astype(jnp.float32) for part in (high, middle, low)]


def relay_kernel(plan_ref, came_ref, _, out_ref, held_ref, sems, *grad_refs):
    peers = plan_ref.shape[1]
    half = came_ref.shape[1] - (EXTRA if grad_refs else 0)

    take = pltpu.make_async_copy(came_ref.at[:, pl.ds(0, half)], held_ref, sems.at[peers])
    take.start()

    def give(q):
        source = jnp.maximum(plan_ref[RELAYED, q], 0)
        return pltpu.make_async_copy(
            held_ref.at[source], out_ref.at[q, pl.ds(half, half)], sems.at[q]
        )

    def turn(q):
        @pl.when(plan_ref[RELAYED, q] >= 0)
        def _():
            give(q).start()

    def wait(q):
        @pl.when(plan_ref[RELAYED, q] >= 0)
        def _():
            give(q).wait()

    if grad_refs:
        (staged_ref,) = grad_refs
        bring = pltpu.make_async_copy(
            came_ref.at[:, pl.ds(half, EXTRA)], staged_ref, sems.at[peers + 1]
        )
        bring.start()
    take.wait()
    each_peer(peers, turn)
    if grad_refs:
        bring.wait()
        sums = jnp.sum(staged_ref[...].astype(jnp.float32), axis=0)
        own = (sums[4:6] + sums[2:4]) + sums[0:2]
        parts = three_parts(own)
        packed = jnp.concatenate(parts + [jnp.zeros((EXTRA - 6, own.shape[1]), jnp.float32)], 0)
        staged_ref[...] = jnp.broadcast_to(packed[None], staged_ref.shape).astype(jnp.bfloat16)
        put = pltpu.make_async_copy(
            staged_ref, out_ref.at[:, pl.ds(2 * half, EXTRA)], sems.at[peers + 2]
        )
        put.start()
        put.wait()
    each_peer(peers, wait)


def relay(plan, came, outgoing, with_grad):
    peers, _, width = came.shape
    scratch = [
        pltpu.VMEM((peers, came.shape[1] - (EXTRA if with_grad else 0), width), came.dtype),
        pltpu.SemaphoreType.DMA((peers + 3,)),
    ]
    if with_grad:
        scratch.append(pltpu.VMEM((peers, EXTRA, width), jnp.bfloat16))
    anywhere = pl.BlockSpec(memory_space=pl.ANY)
    return pl.pallas_call(
        relay_kernel,
        grid_spec=pltpu.PrefetchScalarGridSpec(
            num_scalar_prefetch=1,
            grid=(1,),
            in_specs=[anywhere, anywhere],
            out_specs=anywhere,
            scratch_shapes=scratch,
        ),
        out_shape=jax.ShapeDtypeStruct(outgoing.shape, outgoing.dtype),
        input_output_aliases={2: 0},
        compiler_params=params(),
    )(plan, came, outgoing)


def early_kernel(plan_ref, slots_ref, first_ref, tiles_ref, start_ref, total_ref, sums_ref):
    step = pl.program_id(0)
    half = tiles_ref.shape[2]
    locals_ = start_ref.shape[0]

    @pl.when(step == 0)
    def _():
        sums_ref[pl.ds(0, locals_)] = start_ref[...]

    @pl.when(step <= slots_ref[LAST, 0])
    def _():
        for at in range(GROUP):
            slot = step * GROUP + at
            remote = slots_ref[COLUMN, slot] == locals_
            row = jnp.where(remote, slots_ref[ROW, slot], locals_)
            sums_ref[row] += jnp.dot(
                tiles_ref[at],
                first_ref[slots_ref[HOME, slot], pl.ds(0, half)],
                preferred_element_type=jnp.float32,
            )

    @pl.when(step == pl.num_programs(0) - 1)
    def _():
        total_ref[...] = sums_ref[pl.ds(0, locals_)]


def early_products(plan, slots, first, tile_values, start):
    slot_total, rows, _ = tile_values.shape
    locals_, _, width = start.shape
    return pl.pallas_call(
        early_kernel,
        grid_spec=pltpu.PrefetchScalarGridSpec(
            num_scalar_prefetch=2,
            grid=(slot_total // GROUP,),
            in_specs=[
                whole(*first.shape),
                pl.BlockSpec(
                    (GROUP, rows, rows // 2),
                    lambda i, plan, slots: (jnp.minimum(i, slots[LAST, 0]), 0, 0),
                ),
                whole(*start.shape),
            ],
            out_specs=whole(*start.shape),
            scratch_shapes=[pltpu.VMEM((locals_ + 1, rows, width), jnp.float32)],
        ),
        out_shape=jax.ShapeDtypeStruct(start.shape, start.dtype),
        compiler_params=params(),
        cost_estimate=pl.CostEstimate(
            flops=slot_total * rows * rows * width, bytes_accessed=12 << 20, transcendentals=0
        ),
    )(plan, slots, first, tile_values, start)


def late_scratch(second, tile_values, start):
    peers, _, width = second.shape
    slot_total, rows, _ = tile_values.shape
    return [
        pltpu.VMEM((start.shape[0] + 1, rows, width), jnp.float32),
        pltpu.VMEM(second.shape, second.dtype),
        pltpu.VMEM((slot_total, rows, rows // 2), tile_values.dtype),
        pltpu.SemaphoreType.DMA((PARTS + slot_total // GROUP + 1,)),
    ]


def late_sums(
    plan_ref,
    slots_ref,
    second_ref,
    tiles_ref,
    start_ref,
    total_ref,
    landed_ref,
    held_ref,
    sems,
    landed=None,
):
    peers = plan_ref.shape[1]
    slot_total, rows, half = held_ref.shape
    locals_ = start_ref.shape[0]
    share = peers // PARTS

    def landing(part):
        piece = pl.ds(part * share, share)
        return pltpu.make_async_copy(second_ref.at[piece], landed_ref.at[piece], sems.at[part])

    def holding(group):
        piece = pl.ds(group * GROUP, GROUP)
        return pltpu.make_async_copy(
            tiles_ref.at[piece, :, pl.ds(half, half)], held_ref.at[piece], sems.at[PARTS + group]
        )

    groups = slot_total // GROUP
    begin = pltpu.make_async_copy(
        start_ref, total_ref.at[pl.ds(0, locals_)], sems.at[PARTS + groups]
    )
    begin.start()
    for part in range(PARTS):
        landing(part).start()
    for group in range(groups):

        @pl.when(group <= slots_ref[LAST, 0])
        def _():
            holding(group).start()

    begin.wait()

    def add(q, carry):
        block = plan_ref[ASKED, q]

        @pl.when(block >= 0)
        def _():
            total_ref[block] += landed_ref[q, pl.ds(0, rows)].astype(jnp.float32)

        return carry

    for part in range(PARTS):
        landing(part).wait()
        lax.fori_loop(part * share, (part + 1) * share, add, 0, unroll=4)

    if landed is not None:
        landed()

    def multiply(group, carry):
        @pl.when(group <= slots_ref[LAST, 0])
        def _():
            holding(group).wait()
            for at in range(GROUP):
                slot = group * GROUP + at
                home = slots_ref[HOME, slot]
                remote = slots_ref[COLUMN, slot] == locals_
                row = jnp.where(remote, slots_ref[ROW, slot], locals_)
                via = plan_ref[CAME_VIA, home]
                source = jnp.where(via >= 0, via, home)
                offset = pl.multiple_of(jnp.where(via >= 0, half, 0), half)
                total_ref[row] += jnp.dot(
                    held_ref[slot],
                    landed_ref[source, pl.ds(offset, half)],
                    preferred_element_type=jnp.float32,
                )

        return carry

    lax.fori_loop(0, groups, multiply, 0)


def layer_kernel(
    plan_ref,
    slots_ref,
    second_ref,
    tiles_ref,
    start_ref,
    weight_ref,
    cotangent_ref,
    hidden_ref,
    upstream_ref,
    out_ref,
    total_ref,
    landed_ref,
    held_ref,
    late_sems,
    grad_ref,
    rows_ref,
    staged_ref,
    gradient_ref,
    result_ref,
    back_ref,
    sems,
):
    locals_ = total_ref.shape[0] - 1
    bring = pltpu.make_async_copy(cotangent_ref, gradient_ref, sems.at[2 * locals_])
    bring.start()
    late_sums(
        plan_ref,
        slots_ref,
        second_ref,
        tiles_ref,
        start_ref,
        total_ref,
        landed_ref,
        held_ref,
        late_sems,
    )
    peers = plan_ref.shape[1]
    half = held_ref.shape[2]
    width = upstream_ref.shape[2]
    weight = weight_ref[...]
    grad_ref[...] = jnp.zeros_like(grad_ref)
    bring.wait()

    def give(k):
        return (
            pltpu.make_async_copy(result_ref.at[k], hidden_ref.at[k], sems.at[k]),
            pltpu.make_async_copy(back_ref.at[k], upstream_ref.at[k], sems.at[locals_ + k]),
        )

    def block_step(k, carry):
        aggregated = total_ref[k].astype(jnp.bfloat16)
        preact = jnp.dot(aggregated, weight, preferred_element_type=jnp.float32)
        sigma = 1.0 / (1.0 + jnp.exp(-preact))
        result_ref[k] = (preact * sigma).astype(jnp.bfloat16)
        delta = (
            gradient_ref[k].astype(jnp.float32) * sigma * (1.0 + preact * (1.0 - sigma))
        ).astype(jnp.bfloat16)
        grad_ref[...] += lax.dot_general(
            aggregated, delta, (((0,), (0,)), ((), ())), preferred_element_type=jnp.float32
        )
        back_ref[k] = lax.dot_general(
            delta, weight, (((1,), (1,)), ((), ())), preferred_element_type=jnp.float32
        ).astype(jnp.bfloat16)
        for copy in give(k):
            copy.start()
        return carry

    lax.fori_loop(0, locals_, block_step, 0, unroll=2)
    start_first(plan_ref, back_ref, out_ref, sems.at[2 * locals_ + 1])
    for side in range(2):
        parts = three_parts(grad_ref[:, side * width : (side + 1) * width])
        for at, part in enumerate(parts):
            rows_ref[:, 2 * at + side, :] = part
    for at in range(6, EXTRA):
        rows_ref[:, at, :] = jnp.zeros((peers, width), jnp.float32)
    staged_ref[...] = rows_ref[...].astype(jnp.bfloat16)
    put = pltpu.make_async_copy(
        staged_ref, out_ref.at[:, pl.ds(half, EXTRA)], sems.at[2 * locals_ + 2]
    )
    put.start()
    for k in range(locals_):
        for copy in give(k):
            copy.wait()
    wait_first(out_ref, half, sems.at[2 * locals_ + 1])
    put.wait()


def layer(plan, slots, second, tile_values, start, weight, cotangent):
    peers, _, width = second.shape
    _, rows, _ = tile_values.shape
    locals_ = start.shape[0]
    hid = weight.shape[1]
    assert width == peers and hid == 2 * width
    anywhere = pl.BlockSpec(memory_space=pl.ANY)
    return pl.pallas_call(
        layer_kernel,
        grid_spec=pltpu.PrefetchScalarGridSpec(
            num_scalar_prefetch=2,
            grid=(1,),
            in_specs=[anywhere, anywhere, anywhere, whole(width, hid), anywhere],
            out_specs=[anywhere, anywhere, anywhere],
            scratch_shapes=late_scratch(second, tile_values, start)
            + [
                pltpu.VMEM((width, hid), jnp.float32),
                pltpu.VMEM((peers, EXTRA, width), jnp.float32),
                pltpu.VMEM((peers, EXTRA, width), jnp.bfloat16),
                pltpu.VMEM((locals_, rows, hid), jnp.bfloat16),
                pltpu.VMEM((locals_, rows, hid), jnp.bfloat16),
                pltpu.VMEM((locals_, rows, width), jnp.bfloat16),
                pltpu.SemaphoreType.DMA((2 * locals_ + 3,)),
            ],
        ),
        out_shape=[
            jax.ShapeDtypeStruct((locals_, rows, hid), jnp.bfloat16),
            jax.ShapeDtypeStruct((locals_, rows, width), jnp.bfloat16),
            jax.ShapeDtypeStruct((peers, rows // 2 + EXTRA, width), jnp.bfloat16),
        ],
        compiler_params=params(),
    )(plan, slots, second, tile_values, start, weight, cotangent)


def last_kernel(
    scale,
    plan_ref,
    slots_ref,
    second_ref,
    tiles_ref,
    start_ref,
    out_ref,
    weight_grad_ref,
    total_ref,
    landed_ref,
    held_ref,
    late_sems,
    rows_ref,
):
    rows = held_ref.shape[1]
    width = out_ref.shape[2]

    def put_rows_together():
        rows_ref[...] = landed_ref[:, pl.ds(rows, EXTRA)].astype(jnp.float32)
        for side in range(2):
            weight_grad_ref[:, side * width : (side + 1) * width] = (
                rows_ref[:, 4 + side, :] + rows_ref[:, 2 + side, :] + rows_ref[:, side, :]
            ) * scale

    late_sums(
        plan_ref,
        slots_ref,
        second_ref,
        tiles_ref,
        start_ref,
        total_ref,
        landed_ref,
        held_ref,
        late_sems,
        put_rows_together,
    )
    out_ref[...] = total_ref[pl.ds(0, out_ref.shape[0])].astype(out_ref.dtype)


def last(plan, slots, second, tile_values, start, scale):
    peers, _, width = second.shape
    _, rows, _ = tile_values.shape
    locals_ = start.shape[0]
    anywhere = pl.BlockSpec(memory_space=pl.ANY)
    return pl.pallas_call(
        functools.partial(last_kernel, scale),
        grid_spec=pltpu.PrefetchScalarGridSpec(
            num_scalar_prefetch=2,
            grid=(1,),
            in_specs=[anywhere, anywhere, anywhere],
            out_specs=[whole(locals_, rows, width), whole(peers, 2 * width)],
            scratch_shapes=late_scratch(second, tile_values, start)
            + [pltpu.VMEM((peers, EXTRA, width), jnp.float32)],
        ),
        out_shape=[
            jax.ShapeDtypeStruct((locals_, rows, width), jnp.bfloat16),
            jax.ShapeDtypeStruct((peers, 2 * width), jnp.float32),
        ],
        compiler_params=params(),
    )(plan, slots, second, tile_values, start)


def on_device(features, weight, cotangent, block_pairs, tile_counts, tile_values):
    peers = lax.axis_size("nodes")
    myself = lax.axis_index("nodes")
    rows = tile_values.shape[1]
    width = features.shape[1]
    hid = weight.shape[1]
    locals_ = features.shape[0] // rows
    count = tile_counts[0]
    slot_ids = jnp.arange(block_pairs.shape[0], dtype=jnp.int32)
    peer_ids = jnp.arange(peers, dtype=jnp.int32)
    row_local = jnp.clip(block_pairs[:, 0] - myself * locals_, 0, locals_ - 1)
    col_blocks = block_pairs[:, 1]
    home = col_blocks // locals_
    column = col_blocks % locals_
    live = slot_ids < count
    remote = live & (home != myself)
    hit = (home[None, :] == peer_ids[:, None]) & remote[None, :]
    wanted = jnp.max(jnp.where(hit, column[None, :], -1), axis=1)
    named_twice = jnp.sum(hit.astype(jnp.int32), axis=1) > 1
    wanted = wanted + jnp.where(named_twice, TWICE, 0)
    everyones = exchange(jnp.broadcast_to(wanted[None, :], (peers, peers)))
    blocks = features.reshape(locals_, rows, width)
    plan, sending = make_plan(myself, everyones, blocks)
    cotangent_blocks = cotangent.reshape(locals_, rows, hid)
    scale = 1.0 / math.sqrt(peers * locals_ * rows)

    def sparse():
        slots = jnp.stack(
            [
                row_local,
                jnp.where(remote, home, myself),
                jnp.where(live & ~remote, column, jnp.where(remote, locals_, locals_ + 1)),
                jnp.broadcast_to((count - 1) // GROUP, row_local.shape),
            ]
        )
        first = exchange(sending)
        outgoing, total = own_products(plan, slots, blocks, tile_values, 0)
        first, outgoing = lax.optimization_barrier((first, outgoing))
        second = exchange(relay(plan, first, outgoing, False))
        total = early_products(plan, slots, first, tile_values, total)
        hidden, upstream, halves = layer(
            plan, slots, second, tile_values, total, weight, cotangent_blocks
        )
        first = exchange(halves)
        outgoing, total = own_products(plan, slots, upstream, tile_values, EXTRA)
        first, outgoing = lax.optimization_barrier((first, outgoing))
        second = exchange(relay(plan, first, outgoing, True))
        total = early_products(plan, slots, first, tile_values, total)
        feature_grad, weight_grad = last(plan, slots, second, tile_values, total, scale)
        return hidden, weight_grad, feature_grad

    def full():
        asked = plan[ASKED]
        asked = jnp.where(asked >= 0, asked % TWICE, -1)
        dest = jnp.where(live, jnp.where(remote, home, peers + column), -1)
        earlier = (home[None, :] == home[:, None]) & (slot_ids[None, :] < slot_ids[:, None])
        again = jnp.any(earlier, axis=1).astype(jnp.int32)
        arrived = exchange(pick(asked, blocks))
        outgoing, total = transposed_products(row_local, dest, again, blocks, tile_values, peers)
        returned = exchange(outgoing)
        total = direct_products(row_local, dest, arrived, tile_values, total)
        hidden, local_grad, upstream, requested = dense(
            asked, returned, total, weight, cotangent_blocks
        )
        row_sum = jnp.sum(exchange(local_grad), axis=0) * scale
        weight_grad = exchange(jnp.broadcast_to(row_sum, local_grad.shape))
        arrived = exchange(requested)
        outgoing, total = transposed_products(row_local, dest, again, upstream, tile_values, peers)
        returned = exchange(outgoing)
        total = direct_products(row_local, dest, arrived, tile_values, total)
        return hidden, weight_grad, finish(asked, returned, total)

    hidden, weight_grad, feature_grad = lax.cond(plan[FITS, 0] > 0, sparse, full)
    return (
        hidden.reshape(locals_ * rows, hid),
        weight_grad,
        feature_grad.reshape(locals_ * rows, width),
    )


def solution(mesh):
    return jax.shard_map(
        on_device,
        mesh=mesh,
        in_specs=(
            P("nodes", None),
            P(),
            P("nodes", None),
            P("nodes", None),
            P("nodes"),
            P("nodes", None, None),
        ),
        out_specs=(P("nodes", None), P(), P("nodes", None)),
        check_vma=False,
    )
```

```python
import functools
import math

import jax
import jax.numpy as jnp
from jax import lax
from jax.experimental import pallas as pl
from jax.experimental.pallas import tpu as pltpu
from jax.sharding import PartitionSpec as P

VMEM_LIMIT = 60 * 1024 * 1024
GROUP = 16
PARTS = 4
EXTRA = 16
TWICE = 64
TURNS = 8


def whole(*shape):
    return pl.BlockSpec(shape, lambda *_: (0,) * len(shape), pipeline_mode=pl.Buffered(1))


def params(limit=VMEM_LIMIT):
    return pltpu.CompilerParams(vmem_limit_bytes=limit)


def send_blocks(asked_ref, blocks_ref, out_ref, sems):
    def copy(q):
        block = jnp.maximum(asked_ref[q], 0)
        return pltpu.make_async_copy(blocks_ref.at[block], out_ref.at[q], sems.at[q])

    def start(q, carry):
        @pl.when(asked_ref[q] >= 0)
        def _():
            copy(q).start()

        return carry

    def wait(q, carry):
        @pl.when(asked_ref[q] >= 0)
        def _():
            copy(q).wait()

        return carry

    peers = asked_ref.shape[0]
    lax.fori_loop(0, peers, start, 0)
    lax.fori_loop(0, peers, wait, 0)


def pick(asked, blocks):
    peers = asked.shape[0]
    locals_, rows, width = blocks.shape
    return pl.pallas_call(
        send_blocks,
        grid_spec=pltpu.PrefetchScalarGridSpec(
            num_scalar_prefetch=1,
            grid=(1,),
            in_specs=[whole(locals_, rows, width)],
            out_specs=pl.BlockSpec(memory_space=pl.ANY),
            scratch_shapes=[pltpu.SemaphoreType.DMA((peers,))],
        ),
        out_shape=jax.ShapeDtypeStruct((peers, rows, width), blocks.dtype),
        compiler_params=params(),
    )(asked, blocks)


def transposed_kernel(
    peers, row_ref, dest_ref, again_ref, blocks_ref, tiles_ref, out_ref, total_ref
):
    step = pl.program_id(0)

    @pl.when(step == 0)
    def _():
        total_ref[...] = jnp.zeros_like(total_ref)

    def visit(at, carry):
        slot = step * GROUP + at
        dest = dest_ref[slot]

        @pl.when(dest >= 0)
        def _():
            row = row_ref[slot]
            product = lax.dot_general(
                tiles_ref[at],
                blocks_ref[row],
                (((0,), (0,)), ((), ())),
                preferred_element_type=jnp.float32,
            )
            remote = dest < peers

            @pl.when(remote & (again_ref[slot] == 0))
            def _():
                out_ref[dest] = product.astype(out_ref.dtype)

            @pl.when(remote & (again_ref[slot] == 1))
            def _():
                out_ref[dest] = (out_ref[dest].astype(jnp.float32) + product).astype(out_ref.dtype)

            @pl.when(jnp.logical_not(remote))
            def _():
                column = dest - peers
                total_ref[column] += product
                total_ref[row] += jnp.dot(
                    tiles_ref[at], blocks_ref[column], preferred_element_type=jnp.float32
                )

        return carry

    lax.fori_loop(0, GROUP, visit, 0)


def transposed_products(row_local, dest, again, blocks, tile_values, peers):
    slots, rows, _ = tile_values.shape
    locals_, _, width = blocks.shape
    return pl.pallas_call(
        functools.partial(transposed_kernel, peers),
        grid_spec=pltpu.PrefetchScalarGridSpec(
            num_scalar_prefetch=3,
            grid=(slots // GROUP,),
            in_specs=[
                whole(locals_, rows, width),
                pl.BlockSpec((GROUP, rows, rows), lambda i, *_: (i, 0, 0)),
            ],
            out_specs=[whole(peers, rows, width), whole(locals_, rows, width)],
        ),
        out_shape=[
            jax.ShapeDtypeStruct((peers, rows, width), blocks.dtype),
            jax.ShapeDtypeStruct((locals_, rows, width), jnp.float32),
        ],
        compiler_params=params(),
        cost_estimate=pl.CostEstimate(
            flops=3 * slots * rows * rows * width, bytes_accessed=24 << 20, transcendentals=0
        ),
    )(row_local, dest, again, blocks, tile_values)


def direct_kernel(peers, row_ref, dest_ref, arrived_ref, tiles_ref, start_ref, total_ref):
    step = pl.program_id(0)

    @pl.when(step == 0)
    def _():
        total_ref[...] = start_ref[...]

    def visit(at, carry):
        slot = step * GROUP + at
        source = dest_ref[slot]

        @pl.when((source >= 0) & (source < peers))
        def _():
            total_ref[row_ref[slot]] += jnp.dot(
                tiles_ref[at], arrived_ref[source], preferred_element_type=jnp.float32
            )

        return carry

    lax.fori_loop(0, GROUP, visit, 0)


def direct_products(row_local, dest, arrived, tile_values, start):
    slots, rows, _ = tile_values.shape
    peers, _, width = arrived.shape
    locals_ = start.shape[0]
    return pl.pallas_call(
        functools.partial(direct_kernel, peers),
        grid_spec=pltpu.PrefetchScalarGridSpec(
            num_scalar_prefetch=2,
            grid=(slots // GROUP,),
            in_specs=[
                whole(peers, rows, width),
                pl.BlockSpec((GROUP, rows, rows), lambda i, *_: (i, 0, 0)),
                whole(locals_, rows, width),
            ],
            out_specs=whole(locals_, rows, width),
        ),
        out_shape=jax.ShapeDtypeStruct((locals_, rows, width), jnp.float32),
        compiler_params=params(),
        cost_estimate=pl.CostEstimate(
            flops=2 * slots * rows * rows * width, bytes_accessed=24 << 20, transcendentals=0
        ),
    )(row_local, dest, arrived, tile_values, start)


def add_returned(asked_ref, returned_ref, start_ref, total_ref, landed_ref, sems):
    def copy(q):
        return pltpu.make_async_copy(returned_ref.at[q], landed_ref.at[q], sems.at[q])

    def start(q, carry):
        @pl.when(asked_ref[q] >= 0)
        def _():
            copy(q).start()

        return carry

    def add(q, carry):
        block = asked_ref[q]

        @pl.when(block >= 0)
        def _():
            copy(q).wait()
            total_ref[block] += landed_ref[q].astype(jnp.float32)

        return carry

    peers = asked_ref.shape[0]
    lax.fori_loop(0, peers, start, 0)
    total_ref[...] = start_ref[...]
    lax.fori_loop(0, peers, add, 0)


def dense_kernel(
    asked_ref,
    returned_ref,
    start_ref,
    weight_ref,
    cotangent_ref,
    hidden_ref,
    grad_ref,
    upstream_ref,
    out_ref,
    total_ref,
    landed_ref,
    sems,
):
    add_returned(asked_ref, returned_ref, start_ref, total_ref, landed_ref, sems)
    grad_ref[...] = jnp.zeros_like(grad_ref)
    weight = weight_ref[...]

    def block_step(k, carry):
        aggregated = total_ref[k].astype(jnp.bfloat16)
        preact = jnp.dot(aggregated, weight, preferred_element_type=jnp.float32)
        sigma = 1.0 / (1.0 + jnp.exp(-preact))
        hidden_ref[k] = (preact * sigma).astype(jnp.bfloat16)
        delta = (
            cotangent_ref[k].astype(jnp.float32) * sigma * (1.0 + preact * (1.0 - sigma))
        ).astype(jnp.bfloat16)
        grad_ref[...] += lax.dot_general(
            aggregated, delta, (((0,), (0,)), ((), ())), preferred_element_type=jnp.float32
        )
        upstream_ref[k] = lax.dot_general(
            delta, weight, (((1,), (1,)), ((), ())), preferred_element_type=jnp.float32
        ).astype(jnp.bfloat16)
        return carry

    lax.fori_loop(0, total_ref.shape[0], block_step, 0)
    send_blocks(asked_ref, upstream_ref, out_ref, sems)


def dense(asked, returned, start, weight, cotangent):
    peers, rows, width = returned.shape
    locals_ = start.shape[0]
    hid = weight.shape[1]
    return pl.pallas_call(
        dense_kernel,
        grid_spec=pltpu.PrefetchScalarGridSpec(
            num_scalar_prefetch=1,
            grid=(1,),
            in_specs=[
                pl.BlockSpec(memory_space=pl.ANY),
                whole(locals_, rows, width),
                whole(width, hid),
                whole(locals_, rows, hid),
            ],
            out_specs=[
                whole(locals_, rows, hid),
                whole(width, hid),
                whole(locals_, rows, width),
                pl.BlockSpec(memory_space=pl.ANY),
            ],
            scratch_shapes=[
                pltpu.VMEM((locals_, rows, width), jnp.float32),
                pltpu.VMEM((peers, rows, width), returned.dtype),
                pltpu.SemaphoreType.DMA((peers,)),
            ],
        ),
        out_shape=[
            jax.ShapeDtypeStruct((locals_, rows, hid), jnp.bfloat16),
            jax.ShapeDtypeStruct((width, hid), jnp.float32),
            jax.ShapeDtypeStruct((locals_, rows, width), jnp.bfloat16),
            jax.ShapeDtypeStruct((peers, rows, width), jnp.bfloat16),
        ],
        compiler_params=params(),
    )(asked, returned, start, weight, cotangent)


def finish_kernel(asked_ref, returned_ref, start_ref, out_ref, total_ref, landed_ref, sems):
    add_returned(asked_ref, returned_ref, start_ref, total_ref, landed_ref, sems)
    out_ref[...] = total_ref[...].astype(out_ref.dtype)


def finish(asked, returned, start):
    peers, rows, width = returned.shape
    locals_ = start.shape[0]
    return pl.pallas_call(
        finish_kernel,
        grid_spec=pltpu.PrefetchScalarGridSpec(
            num_scalar_prefetch=1,
            grid=(1,),
            in_specs=[pl.BlockSpec(memory_space=pl.ANY), whole(locals_, rows, width)],
            out_specs=whole(locals_, rows, width),
            scratch_shapes=[
                pltpu.VMEM((locals_, rows, width), jnp.float32),
                pltpu.VMEM((peers, rows, width), returned.dtype),
                pltpu.SemaphoreType.DMA((peers,)),
            ],
        ),
        out_shape=jax.ShapeDtypeStruct((locals_, rows, width), jnp.bfloat16),
        compiler_params=params(),
    )(asked, returned, start)


def exchange(values):
    return lax.all_to_all(values, "nodes", split_axis=0, concat_axis=0, tiled=True)


ASKED, SOURCE, RELAYED, CAME_VIA, WANTED, FITS = range(6)
OPEN = -2


def plan_kernel(
    me_ref, wanted_ref, blocks_ref, plan_ref, out_ref, free_ref, columns_ref, known_ref, sems
):
    peers = wanted_ref.shape[0]
    groups = peers // 8
    me = me_ref[0]
    raw = wanted_ref[...]
    u_ids = lax.broadcasted_iota(jnp.int32, raw.shape, 0)
    named = (raw >= 0).astype(jnp.float32)
    flipped = named.T
    skewed = flipped
    for bit in range(peers.bit_length() - 1):
        turned = pltpu.roll(skewed, peers - (1 << bit), 1)
        skewed = jnp.where(((u_ids >> bit) & 1) == 1, turned, skewed)
    free = (1.0 - skewed.T).astype(jnp.int32)
    free_ref[...] = jnp.broadcast_to(free[:, None, :], free_ref.shape)
    route = jnp.where((named > 0) & (flipped > 0), OPEN, -1)
    spare = 1 - flipped.astype(jnp.int32)
    needs = jnp.sum((route == OPEN).astype(jnp.float32), axis=1, keepdims=True).astype(jnp.int32)
    ranks = (peers - needs) * 8 + (u_ids & 7)
    ranks = [ranks[8 * group : 8 * group + 8] for group in range(groups)]
    lowest = 16 * peers
    v_ids = lax.broadcasted_iota(jnp.int32, (8, peers), 1)

    def left_open(routes):
        count = (routes[0] == OPEN).astype(jnp.float32)
        for part in routes[1:]:
            count += (part == OPEN).astype(jnp.float32)
        return jnp.sum(count).astype(jnp.int32)

    def one(turn, routes, spares):
        shifts = [(turn + 8 * group) & (peers - 1) for group in range(groups)]
        rooms = [free_ref[shift] for shift in shifts]
        next_routes, next_spares, taken = [], [], []
        for route, spare, rank, shift, room in zip(routes, spares, ranks, shifts, rooms):
            fits = (route == OPEN) & ((spare & room) > 0)
            first = jnp.min(jnp.where(fits, rank, lowest), axis=0, keepdims=True)
            chosen = fits & (rank == first)
            taken.append(jnp.where(first < lowest, 0, room))
            next_routes.append(jnp.where(chosen, (v_ids + shift) & (peers - 1), route))
            next_spares.append(pltpu.roll(jnp.where(chosen, 0, spare), peers - 1, 1))
        for shift, room in zip(shifts, taken):
            free_ref[shift] = room
        return tuple(next_routes), tuple(next_spares)

    def some(carry):
        turn, _, routes, spares = carry
        for ahead in range(TURNS):
            routes, spares = one(turn + ahead, routes, spares)
        return turn + TURNS, left_open(routes), routes, spares

    routes = tuple(route[8 * group : 8 * group + 8] for group in range(groups))
    spares = tuple(
        pltpu.roll(spare[8 * group : 8 * group + 8], (peers - 8 * group) % peers, 1)
        for group in range(groups)
    )
    _, left, routes, _ = lax.while_loop(
        lambda carry: (carry[0] < peers) & (carry[1] > 0),
        some,
        (jnp.int32(0), left_open(routes), routes, spares),
    )
    route = jnp.concatenate(routes, 0)
    columns = route.astype(jnp.float32).T.astype(jnp.int32)
    columns_ref[...] = columns
    plan_ref[CAME_VIA : CAME_VIA + 1, :] = columns_ref[pl.ds(me, 1), :]
    plan_ref[RELAYED : RELAYED + 1, :] = jnp.max(
        jnp.where(route == me, u_ids, -1), axis=0, keepdims=True
    )
    columns_ref[...] = raw.astype(jnp.float32).T.astype(jnp.int32)
    asked = columns_ref[pl.ds(me, 1), :]
    plan_ref[ASKED : ASKED + 1, :] = asked
    lanes = lax.broadcasted_iota(jnp.int32, raw.shape, 1)
    my_column = lanes == me
    my_vias = jnp.sum(jnp.where(my_column, columns, 0).astype(jnp.float32), 1, keepdims=True)
    my_asked = jnp.sum(jnp.where(my_column, raw, 0).astype(jnp.float32), 1, keepdims=True)
    second = jnp.where(my_vias == lanes.astype(jnp.float32), 2.0 * my_asked + 1.0, 0.0)
    second = jnp.max(second, axis=0, keepdims=True).astype(jnp.int32)
    pieces = 2 * blocks_ref.shape[0]
    plan_ref[SOURCE : SOURCE + 1, :] = jnp.where(asked >= 0, 2 * asked, second) & (pieces - 1)
    plan_ref[WANTED : WANTED + 1, :] = wanted_ref[pl.ds(me, 1), :]
    twice = jnp.sum((raw >= TWICE).astype(jnp.float32)).astype(jnp.int32)
    fits = jnp.where((left == 0) & (twice == 0), 1, 0)
    plan_ref[FITS:, :] = jnp.full((plan_ref.shape[0] - FITS, peers), fits, jnp.int32)
    tell = pltpu.make_async_copy(plan_ref, known_ref, sems.at[0])
    tell.start()
    tell.wait()
    start_first(known_ref, blocks_ref, out_ref, sems.at[1])
    wait_first(out_ref, blocks_ref.shape[1] // 2, sems.at[1])


def make_plan(myself, wanted, blocks):
    peers = wanted.shape[0]
    locals_, rows, width = blocks.shape
    square = pltpu.VMEM((peers, peers), jnp.int32)
    return pl.pallas_call(
        plan_kernel,
        grid_spec=pltpu.PrefetchScalarGridSpec(
            num_scalar_prefetch=1,
            grid=(1,),
            in_specs=[whole(peers, peers), whole(locals_, rows, width)],
            out_specs=[whole(8, peers), pl.BlockSpec(memory_space=pl.ANY)],
            scratch_shapes=[
                pltpu.VMEM((peers, 8, peers), jnp.int32),
                square,
                pltpu.SMEM((8, peers), jnp.int32),
                pltpu.SemaphoreType.DMA((2,)),
            ],
        ),
        out_shape=[
            jax.ShapeDtypeStruct((8, peers), jnp.int32),
            jax.ShapeDtypeStruct((peers, rows // 2, width), blocks.dtype),
        ],
        compiler_params=params(),
    )(jnp.full((1,), myself, jnp.int32), wanted, blocks)


def each_peer(peers, act):
    def step(q, carry):
        act(q)
        return carry

    lax.fori_loop(0, peers, step, 0, unroll=32)


def start_first(plan_ref, blocks_ref, out_ref, sem):
    half = blocks_ref.shape[1] // 2

    def start(q):
        source = plan_ref[SOURCE, q]
        offset = pl.multiple_of((source & 1) * half, half)
        pltpu.make_async_copy(
            blocks_ref.at[source >> 1, pl.ds(offset, half)], out_ref.at[q, pl.ds(0, half)], sem
        ).start()

    each_peer(plan_ref.shape[1], start)


def wait_first(out_ref, half, sem):
    whole_part = out_ref.at[:, pl.ds(0, half)]
    pltpu.make_async_copy(whole_part, whole_part, sem).wait()


def tiles_spec(rows):
    return pl.BlockSpec(
        (GROUP, rows, rows), lambda i, plan, slots: (jnp.minimum(i, slots[3, 0]), 0, 0)
    )


ROW, HOME, COLUMN, LAST = range(4)


def products_kernel(plan_ref, slots_ref, blocks_ref, tiles_ref, out_ref, total_ref):
    step = pl.program_id(0)
    peers = plan_ref.shape[1]
    rows = blocks_ref.shape[1]
    half = rows // 2
    locals_ = blocks_ref.shape[0]

    @pl.when(step == 0)
    def _():
        total_ref[...] = jnp.zeros_like(total_ref)

        def second_half(q):
            @pl.when((plan_ref[ASKED, q] >= 0) & (plan_ref[WANTED, q] < 0))
            def _():
                out_ref[q, pl.ds(0, half)] = blocks_ref[plan_ref[ASKED, q], pl.ds(half, half)]

        each_peer(peers, second_half)

    @pl.when(step <= slots_ref[LAST, 0])
    def _():
        for at in range(GROUP):
            slot = step * GROUP + at
            row, home, column = slots_ref[ROW, slot], slots_ref[HOME, slot], slots_ref[COLUMN, slot]
            tile = tiles_ref[at]
            product = lax.dot_general(
                tile, blocks_ref[row], (((0,), (0,)), ((), ())), preferred_element_type=jnp.float32
            )
            out_ref[home, pl.ds(0, rows)] = product.astype(out_ref.dtype)

            @pl.when(column < locals_)
            def _():
                total_ref[column] += product
                total_ref[row] += jnp.dot(
                    tile, blocks_ref[column], preferred_element_type=jnp.float32
                )


def own_products(plan, slots, blocks, tile_values, extra):
    peers = plan.shape[1]
    slot_total, rows, _ = tile_values.shape
    locals_, _, width = blocks.shape
    return pl.pallas_call(
        products_kernel,
        grid_spec=pltpu.PrefetchScalarGridSpec(
            num_scalar_prefetch=2,
            grid=(slot_total // GROUP,),
            in_specs=[whole(locals_, rows, width), tiles_spec(rows)],
            out_specs=[whole(peers, rows + extra, width), whole(locals_, rows, width)],
        ),
        out_shape=[
            jax.ShapeDtypeStruct((peers, rows + extra, width), blocks.dtype),
            jax.ShapeDtypeStruct((locals_, rows, width), jnp.float32),
        ],
        compiler_params=params(),
        cost_estimate=pl.CostEstimate(
            flops=3 * slot_total * rows * rows * width, bytes_accessed=24 << 20, transcendentals=0
        ),
    )(plan, slots, blocks, tile_values)


def three_parts(value):
    high = value.astype(jnp.bfloat16)
    rest = value - high.astype(jnp.float32)
    middle = rest.astype(jnp.bfloat16)
    low = (rest - middle.astype(jnp.float32)).astype(jnp.bfloat16)
    return [part.astype(jnp.float32) for part in (high, middle, low)]


def relay_kernel(plan_ref, came_ref, _, out_ref, held_ref, sems, *grad_refs):
    peers = plan_ref.shape[1]
    half = came_ref.shape[1] - (EXTRA if grad_refs else 0)

    take = pltpu.make_async_copy(came_ref.at[:, pl.ds(0, half)], held_ref, sems.at[peers])
    take.start()

    def give(q):
        source = jnp.maximum(plan_ref[RELAYED, q], 0)
        return pltpu.make_async_copy(
            held_ref.at[source], out_ref.at[q, pl.ds(half, half)], sems.at[q]
        )

    def turn(q):
        @pl.when(plan_ref[RELAYED, q] >= 0)
        def _():
            give(q).start()

    def wait(q):
        @pl.when(plan_ref[RELAYED, q] >= 0)
        def _():
            give(q).wait()

    if grad_refs:
        (staged_ref,) = grad_refs
        bring = pltpu.make_async_copy(
            came_ref.at[:, pl.ds(half, EXTRA)], staged_ref, sems.at[peers + 1]
        )
        bring.start()
    take.wait()
    each_peer(peers, turn)
    if grad_refs:
        bring.wait()
        sums = jnp.sum(staged_ref[...].astype(jnp.float32), axis=0)
        own = (sums[4:6] + sums[2:4]) + sums[0:2]
        parts = three_parts(own)
        packed = jnp.concatenate(parts + [jnp.zeros((EXTRA - 6, own.shape[1]), jnp.float32)], 0)
        staged_ref[...] = jnp.broadcast_to(packed[None], staged_ref.shape).astype(jnp.bfloat16)
        put = pltpu.make_async_copy(
            staged_ref, out_ref.at[:, pl.ds(2 * half, EXTRA)], sems.at[peers + 2]
        )
        put.start()
        put.wait()
    each_peer(peers, wait)


def relay(plan, came, outgoing, with_grad):
    peers, _, width = came.shape
    scratch = [
        pltpu.VMEM((peers, came.shape[1] - (EXTRA if with_grad else 0), width), came.dtype),
        pltpu.SemaphoreType.DMA((peers + 3,)),
    ]
    if with_grad:
        scratch.append(pltpu.VMEM((peers, EXTRA, width), jnp.bfloat16))
    anywhere = pl.BlockSpec(memory_space=pl.ANY)
    return pl.pallas_call(
        relay_kernel,
        grid_spec=pltpu.PrefetchScalarGridSpec(
            num_scalar_prefetch=1,
            grid=(1,),
            in_specs=[anywhere, anywhere],
            out_specs=anywhere,
            scratch_shapes=scratch,
        ),
        out_shape=jax.ShapeDtypeStruct(outgoing.shape, outgoing.dtype),
        input_output_aliases={2: 0},
        compiler_params=params(),
    )(plan, came, outgoing)


def early_kernel(plan_ref, slots_ref, first_ref, tiles_ref, start_ref, total_ref, sums_ref):
    step = pl.program_id(0)
    half = tiles_ref.shape[2]
    locals_ = start_ref.shape[0]

    @pl.when(step == 0)
    def _():
        sums_ref[pl.ds(0, locals_)] = start_ref[...]

    @pl.when(step <= slots_ref[LAST, 0])
    def _():
        for at in range(GROUP):
            slot = step * GROUP + at
            remote = slots_ref[COLUMN, slot] == locals_
            row = jnp.where(remote, slots_ref[ROW, slot], locals_)
            sums_ref[row] += jnp.dot(
                tiles_ref[at],
                first_ref[slots_ref[HOME, slot], pl.ds(0, half)],
                preferred_element_type=jnp.float32,
            )

    @pl.when(step == pl.num_programs(0) - 1)
    def _():
        total_ref[...] = sums_ref[pl.ds(0, locals_)]


def early_products(plan, slots, first, tile_values, start):
    slot_total, rows, _ = tile_values.shape
    locals_, _, width = start.shape
    return pl.pallas_call(
        early_kernel,
        grid_spec=pltpu.PrefetchScalarGridSpec(
            num_scalar_prefetch=2,
            grid=(slot_total // GROUP,),
            in_specs=[
                whole(*first.shape),
                pl.BlockSpec(
                    (GROUP, rows, rows // 2),
                    lambda i, plan, slots: (jnp.minimum(i, slots[LAST, 0]), 0, 0),
                ),
                whole(*start.shape),
            ],
            out_specs=whole(*start.shape),
            scratch_shapes=[pltpu.VMEM((locals_ + 1, rows, width), jnp.float32)],
        ),
        out_shape=jax.ShapeDtypeStruct(start.shape, start.dtype),
        compiler_params=params(),
        cost_estimate=pl.CostEstimate(
            flops=slot_total * rows * rows * width, bytes_accessed=12 << 20, transcendentals=0
        ),
    )(plan, slots, first, tile_values, start)


def late_scratch(second, tile_values, start):
    peers, _, width = second.shape
    slot_total, rows, _ = tile_values.shape
    return [
        pltpu.VMEM((start.shape[0] + 1, rows, width), jnp.float32),
        pltpu.VMEM(second.shape, second.dtype),
        pltpu.VMEM((slot_total, rows, rows // 2), tile_values.dtype),
        pltpu.SemaphoreType.DMA((PARTS + slot_total // GROUP + 1,)),
    ]


def late_sums(
    plan_ref,
    slots_ref,
    second_ref,
    tiles_ref,
    start_ref,
    total_ref,
    landed_ref,
    held_ref,
    sems,
    landed=None,
):
    peers = plan_ref.shape[1]
    slot_total, rows, half = held_ref.shape
    locals_ = start_ref.shape[0]
    share = peers // PARTS

    def landing(part):
        piece = pl.ds(part * share, share)
        return pltpu.make_async_copy(second_ref.at[piece], landed_ref.at[piece], sems.at[part])

    def holding(group):
        piece = pl.ds(group * GROUP, GROUP)
        return pltpu.make_async_copy(
            tiles_ref.at[piece, :, pl.ds(half, half)], held_ref.at[piece], sems.at[PARTS + group]
        )

    groups = slot_total // GROUP
    begin = pltpu.make_async_copy(
        start_ref, total_ref.at[pl.ds(0, locals_)], sems.at[PARTS + groups]
    )
    begin.start()
    for part in range(PARTS):
        landing(part).start()
    for group in range(groups):

        @pl.when(group <= slots_ref[LAST, 0])
        def _():
            holding(group).start()

    begin.wait()

    def add(q, carry):
        block = plan_ref[ASKED, q]

        @pl.when(block >= 0)
        def _():
            total_ref[block] += landed_ref[q, pl.ds(0, rows)].astype(jnp.float32)

        return carry

    for part in range(PARTS):
        landing(part).wait()
        lax.fori_loop(part * share, (part + 1) * share, add, 0, unroll=8)

    if landed is not None:
        landed()

    def multiply(group, carry):
        @pl.when(group <= slots_ref[LAST, 0])
        def _():
            holding(group).wait()
            for at in range(GROUP):
                slot = group * GROUP + at
                home = slots_ref[HOME, slot]
                remote = slots_ref[COLUMN, slot] == locals_
                row = jnp.where(remote, slots_ref[ROW, slot], locals_)
                via = plan_ref[CAME_VIA, home]
                source = jnp.where(via >= 0, via, home)
                offset = pl.multiple_of(jnp.where(via >= 0, half, 0), half)
                total_ref[row] += jnp.dot(
                    held_ref[slot],
                    landed_ref[source, pl.ds(offset, half)],
                    preferred_element_type=jnp.float32,
                )

        return carry

    lax.fori_loop(0, groups, multiply, 0)


def layer_kernel(
    plan_ref,
    slots_ref,
    second_ref,
    tiles_ref,
    start_ref,
    weight_ref,
    cotangent_ref,
    hidden_ref,
    upstream_ref,
    out_ref,
    total_ref,
    landed_ref,
    held_ref,
    late_sems,
    grad_ref,
    rows_ref,
    staged_ref,
    gradient_ref,
    result_ref,
    back_ref,
    sems,
):
    locals_ = total_ref.shape[0] - 1
    bring = pltpu.make_async_copy(cotangent_ref, gradient_ref, sems.at[2 * locals_])
    bring.start()
    late_sums(
        plan_ref,
        slots_ref,
        second_ref,
        tiles_ref,
        start_ref,
        total_ref,
        landed_ref,
        held_ref,
        late_sems,
    )
    peers = plan_ref.shape[1]
    half = held_ref.shape[2]
    width = upstream_ref.shape[2]
    weight = weight_ref[...]
    grad_ref[...] = jnp.zeros_like(grad_ref)
    bring.wait()

    def give(k):
        return (
            pltpu.make_async_copy(result_ref.at[k], hidden_ref.at[k], sems.at[k]),
            pltpu.make_async_copy(back_ref.at[k], upstream_ref.at[k], sems.at[locals_ + k]),
        )

    def block_step(k, carry):
        aggregated = total_ref[k].astype(jnp.bfloat16)
        preact = jnp.dot(aggregated, weight, preferred_element_type=jnp.float32)
        sigma = 1.0 / (1.0 + jnp.exp(-preact))
        result_ref[k] = (preact * sigma).astype(jnp.bfloat16)
        delta = (
            gradient_ref[k].astype(jnp.float32) * sigma * (1.0 + preact * (1.0 - sigma))
        ).astype(jnp.bfloat16)
        grad_ref[...] += lax.dot_general(
            aggregated, delta, (((0,), (0,)), ((), ())), preferred_element_type=jnp.float32
        )
        back_ref[k] = lax.dot_general(
            delta, weight, (((1,), (1,)), ((), ())), preferred_element_type=jnp.float32
        ).astype(jnp.bfloat16)
        for copy in give(k):
            copy.start()
        return carry

    lax.fori_loop(0, locals_, block_step, 0, unroll=4)
    start_first(plan_ref, back_ref, out_ref, sems.at[2 * locals_ + 1])
    for side in range(2):
        parts = three_parts(grad_ref[:, side * width : (side + 1) * width])
        for at, part in enumerate(parts):
            rows_ref[:, 2 * at + side, :] = part
    for at in range(6, EXTRA):
        rows_ref[:, at, :] = jnp.zeros((peers, width), jnp.float32)
    staged_ref[...] = rows_ref[...].astype(jnp.bfloat16)
    put = pltpu.make_async_copy(
        staged_ref, out_ref.at[:, pl.ds(half, EXTRA)], sems.at[2 * locals_ + 2]
    )
    put.start()
    for k in range(locals_):
        for copy in give(k):
            copy.wait()
    wait_first(out_ref, half, sems.at[2 * locals_ + 1])
    put.wait()


def layer(plan, slots, second, tile_values, start, weight, cotangent):
    peers, _, width = second.shape
    _, rows, _ = tile_values.shape
    locals_ = start.shape[0]
    hid = weight.shape[1]
    assert width == peers and hid == 2 * width
    anywhere = pl.BlockSpec(memory_space=pl.ANY)
    return pl.pallas_call(
        layer_kernel,
        grid_spec=pltpu.PrefetchScalarGridSpec(
            num_scalar_prefetch=2,
            grid=(1,),
            in_specs=[anywhere, anywhere, anywhere, whole(width, hid), anywhere],
            out_specs=[anywhere, anywhere, anywhere],
            scratch_shapes=late_scratch(second, tile_values, start)
            + [
                pltpu.VMEM((width, hid), jnp.float32),
                pltpu.VMEM((peers, EXTRA, width), jnp.float32),
                pltpu.VMEM((peers, EXTRA, width), jnp.bfloat16),
                pltpu.VMEM((locals_, rows, hid), jnp.bfloat16),
                pltpu.VMEM((locals_, rows, hid), jnp.bfloat16),
                pltpu.VMEM((locals_, rows, width), jnp.bfloat16),
                pltpu.SemaphoreType.DMA((2 * locals_ + 3,)),
            ],
        ),
        out_shape=[
            jax.ShapeDtypeStruct((locals_, rows, hid), jnp.bfloat16),
            jax.ShapeDtypeStruct((locals_, rows, width), jnp.bfloat16),
            jax.ShapeDtypeStruct((peers, rows // 2 + EXTRA, width), jnp.bfloat16),
        ],
        compiler_params=params(),
    )(plan, slots, second, tile_values, start, weight, cotangent)


def last_kernel(
    scale,
    plan_ref,
    slots_ref,
    second_ref,
    tiles_ref,
    start_ref,
    out_ref,
    weight_grad_ref,
    total_ref,
    landed_ref,
    held_ref,
    late_sems,
    rows_ref,
):
    rows = held_ref.shape[1]
    width = out_ref.shape[2]

    def put_rows_together():
        rows_ref[...] = landed_ref[:, pl.ds(rows, EXTRA)].astype(jnp.float32)
        for side in range(2):
            weight_grad_ref[:, side * width : (side + 1) * width] = (
                rows_ref[:, 4 + side, :] + rows_ref[:, 2 + side, :] + rows_ref[:, side, :]
            ) * scale

    late_sums(
        plan_ref,
        slots_ref,
        second_ref,
        tiles_ref,
        start_ref,
        total_ref,
        landed_ref,
        held_ref,
        late_sems,
        put_rows_together,
    )
    out_ref[...] = total_ref[pl.ds(0, out_ref.shape[0])].astype(out_ref.dtype)


def last(plan, slots, second, tile_values, start, scale):
    peers, _, width = second.shape
    _, rows, _ = tile_values.shape
    locals_ = start.shape[0]
    anywhere = pl.BlockSpec(memory_space=pl.ANY)
    return pl.pallas_call(
        functools.partial(last_kernel, scale),
        grid_spec=pltpu.PrefetchScalarGridSpec(
            num_scalar_prefetch=2,
            grid=(1,),
            in_specs=[anywhere, anywhere, anywhere],
            out_specs=[whole(locals_, rows, width), whole(peers, 2 * width)],
            scratch_shapes=late_scratch(second, tile_values, start)
            + [pltpu.VMEM((peers, EXTRA, width), jnp.float32)],
        ),
        out_shape=[
            jax.ShapeDtypeStruct((locals_, rows, width), jnp.bfloat16),
            jax.ShapeDtypeStruct((peers, 2 * width), jnp.float32),
        ],
        compiler_params=params(),
    )(plan, slots, second, tile_values, start)


def on_device(features, weight, cotangent, block_pairs, tile_counts, tile_values):
    peers = lax.axis_size("nodes")
    myself = lax.axis_index("nodes")
    rows = tile_values.shape[1]
    width = features.shape[1]
    hid = weight.shape[1]
    locals_ = features.shape[0] // rows
    count = tile_counts[0]
    slot_ids = jnp.arange(block_pairs.shape[0], dtype=jnp.int32)
    peer_ids = jnp.arange(peers, dtype=jnp.int32)
    row_local = jnp.clip(block_pairs[:, 0] - myself * locals_, 0, locals_ - 1)
    col_blocks = block_pairs[:, 1]
    home = col_blocks // locals_
    column = col_blocks % locals_
    live = slot_ids < count
    remote = live & (home != myself)
    hit = (home[None, :] == peer_ids[:, None]) & remote[None, :]
    wanted = jnp.max(jnp.where(hit, column[None, :], -1), axis=1)
    named_twice = jnp.sum(hit.astype(jnp.int32), axis=1) > 1
    wanted = wanted + jnp.where(named_twice, TWICE, 0)
    everyones = exchange(jnp.broadcast_to(wanted[None, :], (peers, peers)))
    blocks = features.reshape(locals_, rows, width)
    plan, sending = make_plan(myself, everyones, blocks)
    cotangent_blocks = cotangent.reshape(locals_, rows, hid)
    scale = 1.0 / math.sqrt(peers * locals_ * rows)

    def sparse():
        slots = jnp.stack(
            [
                row_local,
                jnp.where(remote, home, myself),
                jnp.where(live & ~remote, column, jnp.where(remote, locals_, locals_ + 1)),
                jnp.broadcast_to((count - 1) // GROUP, row_local.shape),
            ]
        )
        first = exchange(sending)
        outgoing, total = own_products(plan, slots, blocks, tile_values, 0)
        first, outgoing = lax.optimization_barrier((first, outgoing))
        second = exchange(relay(plan, first, outgoing, False))
        total = early_products(plan, slots, first, tile_values, total)
        hidden, upstream, halves = layer(
            plan, slots, second, tile_values, total, weight, cotangent_blocks
        )
        first = exchange(halves)
        outgoing, total = own_products(plan, slots, upstream, tile_values, EXTRA)
        first, outgoing = lax.optimization_barrier((first, outgoing))
        second = exchange(relay(plan, first, outgoing, True))
        total = early_products(plan, slots, first, tile_values, total)
        feature_grad, weight_grad = last(plan, slots, second, tile_values, total, scale)
        return hidden, weight_grad, feature_grad

    def full():
        asked = plan[ASKED]
        asked = jnp.where(asked >= 0, asked % TWICE, -1)
        dest = jnp.where(live, jnp.where(remote, home, peers + column), -1)
        earlier = (home[None, :] == home[:, None]) & (slot_ids[None, :] < slot_ids[:, None])
        again = jnp.any(earlier, axis=1).astype(jnp.int32)
        arrived = exchange(pick(asked, blocks))
        outgoing, total = transposed_products(row_local, dest, again, blocks, tile_values, peers)
        returned = exchange(outgoing)
        total = direct_products(row_local, dest, arrived, tile_values, total)
        hidden, local_grad, upstream, requested = dense(
            asked, returned, total, weight, cotangent_blocks
        )
        row_sum = jnp.sum(exchange(local_grad), axis=0) * scale
        weight_grad = exchange(jnp.broadcast_to(row_sum, local_grad.shape))
        arrived = exchange(requested)
        outgoing, total = transposed_products(row_local, dest, again, upstream, tile_values, peers)
        returned = exchange(outgoing)
        total = direct_products(row_local, dest, arrived, tile_values, total)
        return hidden, weight_grad, finish(asked, returned, total)

    hidden, weight_grad, feature_grad = lax.cond(plan[FITS, 0] > 0, sparse, full)
    return (
        hidden.reshape(locals_ * rows, hid),
        weight_grad,
        feature_grad.reshape(locals_ * rows, width),
    )


def solution(mesh):
    return jax.shard_map(
        on_device,
        mesh=mesh,
        in_specs=(
            P("nodes", None),
            P(),
            P("nodes", None),
            P("nodes", None),
            P("nodes"),
            P("nodes", None, None),
        ),
        out_specs=(P("nodes", None), P(), P("nodes", None)),
        check_vma=False,
    )
```
